32 devices in a mesh: tm: 4 (over y, x), space: 8 (over z, core).
Axes of the slice: x: 2, y: 2, z: 4, core: 2. Of those that a mesh axis runs over, the one named last changes fastest.
Arguments:
- conserved_field: float32 [16, 10, 64, 1024], P('tm', None, None, 'space'), may hold values from -6 to 6
- face_neighbours: int32 [2, 1024], P(None, 'space'), may hold values from 0 to 1023, as said below
- counterpart_group: int32 [16], P('tm'), may hold values from 0 to 7
- counterpart_shift: int32 [16], P('tm'), may hold values from 0 to 127
- volume_operator: float32 [2, 64, 64], replicated, may hold values from -0.75 to 0.75
- flux_matrix: float32 [2, 10, 10], replicated, may hold values from -2 to 2
Outputs:
- new_state: float32 [16, 10, 64, 1024], P('tm', None, None, 'space')
- last_residual: float32 [16, 10, 64, 1024], P('tm', None, None, 'space')
The draws below stay inside these ranges and needn't reach their ends.
Inputs may be any that keep to these rules, and one draw needn't show every extreme that they name: face_neighbours[0, e] = (e - d) mod 1024 and face_neighbours[1, e] = (e + d2) mod 1024 with 1 <= d, d2 <= 4; both distances 4 occur.
All inputs are finite; a program needn't handle non-finite values.
Results may differ from the reference program's by a relative error of at most 0.0001.
Values sent between devices are 32-bit elements; how exact they have to be, the bound alone decides.
No kernel may reach another device: no remote copies, remote signals or barrier semaphores. Data moves between devices by JAX's collectives and lax.ppermute only.
A program may use at most 64 MiB of HBM per device.

```python
import jax
import jax.numpy as jnp
from jax import lax

SAMPLE_COUNT = 16
UNKNOWN_COUNT = 10
NODE_COUNT = 64
REACH = 4
ITERS = 2
CELLS_PER_SPLIT = 128
CELL_TOTAL = 1024
GROUP_COUNT = 8


def draw_face_neighbours(key, part):
    first_key, second_key = jax.random.split(jax.random.fold_in(key, 11))
    back_gap = jax.random.randint(first_key, (CELL_TOTAL,), 1, REACH + 1)
    ahead_gap = jax.random.randint(second_key, (CELL_TOTAL,), 1, REACH + 1)
    back_gap = back_gap.at[0].set(REACH)
    ahead_gap = ahead_gap.at[CELL_TOTAL - 1].set(REACH)
    elem_index = jnp.arange(CELL_TOTAL, dtype=jnp.int32)
    lower_side = (elem_index - back_gap) % CELL_TOTAL
    upper_side = (elem_index + ahead_gap) % CELL_TOTAL
    return jnp.stack([lower_side, upper_side]).astype(jnp.int32)


def place_ends(array, own_key, smallest, top_value):
    extent = array.shape
    spot = [jax.random.randint(jax.random.fold_in(own_key, axis), (), 0, extent[axis]) for axis in range(len(extent))]
    array = array.at[tuple(spot)].set(smallest)
    longest = extent.index(max(extent))
    spot[longest] = (spot[longest] + 1) % extent[longest]
    return array.at[tuple(spot)].set(top_value)


def steps_of(rng, dims, cuts, least, largest):
    def one(dim, shards_of):
        draws = jax.random.uniform(jax.random.fold_in(jax.random.fold_in(rng, 6), dim), (shards_of,), jnp.float32, least / len(cuts), largest / len(cuts))
        return jnp.repeat(jnp.exp(draws), dims[dim] // shards_of).reshape((-1,) + (1,) * (len(dims) - dim - 1))

    level = one(*cuts[0])
    for cut in cuts[1:]:
        level = level * one(*cut)
    return level


def normal_values(own_key, extent, deviation, bound, pieces=(), kind=jnp.bfloat16):
    gain = steps_of(own_key, extent, pieces, -0.22, 0.18) if pieces else 1.0
    array = jax.random.normal(own_key, extent, jnp.float32) * deviation * gain
    return jnp.minimum(jnp.maximum(array, -bound), bound).astype(kind)


def setup_inputs(seed: int = 0) -> dict:
    seeds = jax.random.split(jax.random.key(seed), 7)
    conserved_field = normal_values(seeds[0], (SAMPLE_COUNT, UNKNOWN_COUNT, NODE_COUNT, CELL_TOTAL), 1.0, 6.0, ((0, 4), (3, 8)), jnp.float32)
    face_neighbours = draw_face_neighbours(jax.random.fold_in(seeds[6], 71), 0)
    counterpart_group = place_ends(jax.random.randint(seeds[2], (SAMPLE_COUNT,), 0, GROUP_COUNT), jax.random.fold_in(seeds[2], 1), 0, GROUP_COUNT - 1).astype(jnp.int32)
    counterpart_shift = place_ends(jax.random.randint(seeds[3], (SAMPLE_COUNT,), 0, CELLS_PER_SPLIT), jax.random.fold_in(seeds[3], 1), 0, CELLS_PER_SPLIT - 1).astype(jnp.int32)
    volume_operator = normal_values(seeds[4], (2, NODE_COUNT, NODE_COUNT), NODE_COUNT ** -0.5, 0.75, (), jnp.float32)
    flux_matrix = normal_values(seeds[5], (2, UNKNOWN_COUNT, UNKNOWN_COUNT), UNKNOWN_COUNT ** -0.5, 2.0, (), jnp.float32)
    return {"conserved_field": conserved_field, "face_neighbours": face_neighbours, "counterpart_group": counterpart_group, "counterpart_shift": counterpart_shift, "volume_operator": volume_operator, "flux_matrix": flux_matrix}


lift_scale = 2.0
dissipation = 1.5
angular_speed = 0.5
damping_factor = 4.0
pseudo_step = 0.2


def face_traces(field):
    inst_count = field.shape[0]
    elem_count = field.shape[-1]
    cube_view = field.reshape(inst_count, UNKNOWN_COUNT, 4, 4, 4, elem_count)
    lower_face = cube_view[:, :, 0].reshape(inst_count, UNKNOWN_COUNT, 16, elem_count)
    upper_face = cube_view[:, :, 3].reshape(inst_count, UNKNOWN_COUNT, 16, elem_count)
    slide_face = cube_view[:, :, :, :, 3].reshape(inst_count, UNKNOWN_COUNT, 16, elem_count)
    return lower_face, upper_face, slide_face


def momentum_turning(boundary_samples, cycle_samples):
    blade_azimuth = 2.0 * jnp.pi * cycle_samples.astype(jnp.float32) / SAMPLE_COUNT
    cosine = jnp.cos(blade_azimuth)[:, None, None]
    sine = jnp.sin(blade_azimuth)[:, None, None]
    first_comp = boundary_samples[:, 1]
    second_comp = boundary_samples[:, 2]
    turned_one = cosine * first_comp - sine * second_comp
    turned_two = sine * first_comp + cosine * second_comp
    return jnp.concatenate([boundary_samples[:, :1], turned_one[:, None], turned_two[:, None], boundary_samples[:, 3:]], axis=1)


def face_term(matrix, normal_sign, outside, inside):
    jump = outside - inside
    mixed = jnp.einsum('vw,twqe->tvqe', matrix, jump, precision=lax.Precision.HIGHEST)
    return 0.5 * lift_scale * (normal_sign * mixed - dissipation * jump)


def assemble(lower_term, upper_term, slide_term):
    inst_count = lower_term.shape[0]
    elem_count = lower_term.shape[-1]
    shaped = (inst_count, UNKNOWN_COUNT, 4, 4, elem_count)
    corrections = jnp.zeros((inst_count, UNKNOWN_COUNT, 4, 4, 4, elem_count), lower_term.dtype)
    corrections = corrections.at[:, :, 0].add(lower_term.reshape(shaped))
    corrections = corrections.at[:, :, 3].add(upper_term.reshape(shaped))
    corrections = corrections.at[:, :, :, :, 3].add(slide_term.reshape(shaped))
    return corrections.reshape(inst_count, UNKNOWN_COUNT, NODE_COUNT, elem_count)


def residual_of(field, face_neighbours, counterpart_group, counterpart_shift, volume_operator, flux_matrix):
    fluxes = jnp.einsum('dvw,twpe->dtvpe', flux_matrix, field, precision=lax.Precision.HIGHEST)
    volume = jnp.einsum('dpq,dtvqe->tvpe', volume_operator, fluxes, precision=lax.Precision.HIGHEST)
    lower_face, upper_face, slide_face = face_traces(field)
    lower_out = jnp.take(upper_face, face_neighbours[0], axis=-1)
    upper_out = jnp.take(lower_face, face_neighbours[1], axis=-1)
    elem_index = jnp.arange(CELL_TOTAL, dtype=jnp.int32)
    partner = (elem_index[None, :] + counterpart_group[:, None] * CELLS_PER_SPLIT + counterpart_shift[:, None]) % CELL_TOTAL
    paired_boundary = jax.vmap(lambda rows_all, picks: jnp.take(rows_all, picks, axis=-1))(slide_face, partner)
    paired_boundary = momentum_turning(paired_boundary, jnp.arange(SAMPLE_COUNT, dtype=jnp.int32))
    corrections = assemble(face_term(flux_matrix[0], -1.0, lower_out, lower_face),
                           face_term(flux_matrix[0], 1.0, upper_out, upper_face),
                           face_term(flux_matrix[1], 1.0, paired_boundary, slide_face))
    frequency_content = jnp.fft.rfft(field, axis=0)
    fourier_wavenumbers = jnp.arange(SAMPLE_COUNT // 2 + 1).astype(jnp.float32)
    damped_signal = angular_speed * fourier_wavenumbers * jnp.exp(-damping_factor * (fourier_wavenumbers / (SAMPLE_COUNT // 2)) ** 8)
    damped_signal = jnp.where(fourier_wavenumbers < SAMPLE_COUNT // 2, damped_signal, 0.0)
    cyclic_signal = jnp.fft.irfft(1j * damped_signal[:, None, None, None] * frequency_content, n=SAMPLE_COUNT, axis=0)
    return volume + corrections + cyclic_signal.astype(field.dtype)


def reference(conserved_field, face_neighbours, counterpart_group, counterpart_shift, volume_operator, flux_matrix):
    field = conserved_field
    residual = jnp.zeros_like(field)
    for sweep_index in range(ITERS):
        residual = residual_of(field, face_neighbours, counterpart_group, counterpart_shift, volume_operator, flux_matrix)
        field = field - pseudo_step * residual
    return field, residual
```

```python
import functools

import jax
import jax.numpy as jnp
import numpy as np
from jax import lax
from jax.experimental import pallas as pl
from jax.experimental.pallas import tpu as pltpu
from jax.sharding import PartitionSpec as P

REACH = 4
ITERS = 2
LIFT = 2.0
DISSIPATION = 1.5
ANGULAR = 0.5
DAMPING = 4.0
STEP = 0.2
SUB = 8

VMEM = pl.BlockSpec(memory_space=pltpu.VMEM)
SMEM = pl.BlockSpec(memory_space=pltpu.SMEM)
F32 = jnp.float32
BF16 = jnp.bfloat16


class Sizes:
    def __init__(self, field_shape):
        self.L, self.V, self.Q, self.E = field_shape
        self.R = self.V * self.Q
        self.M = lax.axis_size("tm")
        self.N = lax.axis_size("space")
        self.T = self.L * self.M
        self.Z = self.N // 2
        self.RC = self.R // self.M
        self.face = self.Q // 4
        self.FR = self.V * self.face
        self.PL = self.Z // self.L
        self.CH = self.FR // self.PL
        self.H = SUB * self.L

    def z_rows(self, j):
        if j == 0:
            return 2 * self.H + self.CH
        return self.CH + self.H * ((j == 1) + (j == self.Z - 1))


def time_weights(total):
    k = np.arange(1, total // 2, dtype=np.float64)
    gains = 2.0 * ANGULAR * k * np.exp(-DAMPING * (k / (total // 2)) ** 8) / total
    lag = np.arange(total, dtype=np.float64)
    return np.sum(gains[:, None] * np.sin(2.0 * np.pi * k[:, None] * lag[None, :] / total), axis=0)


def call(body, outs, ins, scratch=(), flops=0, nbytes=0):
    return pl.pallas_call(
        body,
        out_shape=outs,
        in_specs=ins,
        out_specs=jax.tree.map(lambda _: VMEM, outs),
        scratch_shapes=list(scratch),
        cost_estimate=pl.CostEstimate(flops=flops, bytes_accessed=nbytes, transcendentals=0),
        compiler_params=pltpu.CompilerParams(vmem_limit_bytes=40 * 1024 * 1024),
    )


def lanes_of(x, index):
    return jnp.take_along_axis(x, index, axis=1, mode="promise_in_bounds")


def split(x):
    hi = x.astype(BF16)
    return hi, (x - hi.astype(F32)).astype(BF16)


def dot3(a_hi, a_lo, x):
    x_hi, x_lo = split(x)
    out = jnp.dot(a_hi, x_hi, preferred_element_type=F32)
    out += jnp.dot(a_hi, x_lo, preferred_element_type=F32)
    return out + jnp.dot(a_lo, x_hi, preferred_element_type=F32)


def iota(shape, axis):
    return lax.broadcasted_iota(jnp.int32, shape, axis)


def matrices(sz, flux, volume_operator):
    V, Q, face = sz.V, sz.Q, sz.face

    def body(flux_ref, vol_ref, in_hi, in_lo, out_hi, out_lo):
        p = iota((Q, Q), 0)
        q = iota((Q, Q), 1)
        same = p == q
        low = same & (p < face)
        up = same & (p >= Q - face)
        slide = same & (p % 4 == 3)
        fp = iota((Q, face), 0)
        fq = iota((Q, face), 1)
        to_low = fp == fq
        to_up = fp == fq + (Q - face)
        to_slide = fp == 4 * fq + 3
        vol0 = vol_ref[0]
        vol1 = vol_ref[1]
        for v in range(V):
            blocks = []
            lows, ups, slides = [], [], []
            for w in range(V):
                f0 = flux_ref[0, v, w]
                f1 = flux_ref[1, v, w]
                d = DISSIPATION if v == w else 0.0
                a_low = 0.5 * LIFT * (-f0 - d)
                a_up = 0.5 * LIFT * (f0 - d)
                a_slide = 0.5 * LIFT * (f1 - d)
                block = f0 * vol0 + f1 * vol1
                block -= jnp.where(low, a_low, 0.0)
                block -= jnp.where(up, a_up, 0.0)
                block -= jnp.where(slide, a_slide, 0.0)
                blocks.append(block)
                lows.append(jnp.where(to_low, a_low, 0.0))
                ups.append(jnp.where(to_up, a_up, 0.0))
                slides.append(jnp.where(to_slide, a_slide, 0.0))
            hi, lo = split(jnp.concatenate(blocks, axis=1))
            in_hi[pl.ds(v * Q, Q), :] = hi
            in_lo[pl.ds(v * Q, Q), :] = lo
            hi, lo = split(jnp.concatenate(lows + ups + slides, axis=1))
            out_hi[pl.ds(v * Q, Q), :] = hi
            out_lo[pl.ds(v * Q, Q), :] = lo

    inner = jax.ShapeDtypeStruct((sz.R, sz.R), BF16)
    outer = jax.ShapeDtypeStruct((sz.R, 3 * sz.FR), BF16)
    nbytes = 4 * sz.R * (sz.R + 3 * sz.FR)
    return call(body, [inner, inner, outer, outer], [SMEM, VMEM], (), nbytes, nbytes)(flux, volume_operator)


def pack_shapes(sz):
    tm = [jax.ShapeDtypeStruct((sz.L, sz.RC, sz.E), F32) for _ in range(sz.M)]
    zz = [jax.ShapeDtypeStruct((sz.z_rows(j), sz.E), F32) for j in range(sz.Z)]
    return tm + zz


def pack_scratch(sz):
    return [pltpu.VMEM((sz.Z, sz.CH, sz.E), F32)]


def pack(sz, where, u_ref, outs, stage):
    tm, zz = outs[: sz.M], outs[sz.M :]
    me, z = where[0], where[1]
    for j in range(sz.M):
        start = pl.multiple_of((me ^ j) * sz.RC, SUB)
        tm[j][...] = u_ref[:, pl.ds(start, sz.RC), :]
    for p in range(sz.Z):
        first = (p % sz.PL) * sz.CH
        stage[p] = u_ref[p // sz.PL, pl.ds(3 + 4 * first, sz.CH, stride=4), :]
    lane = iota((SUB, sz.E), 1)
    slot = lane // REACH
    last = sz.E - REACH + lane % REACH
    first = lane % REACH
    tiles = sz.face // SUB
    halos = []
    for l in range(sz.L):
        up = jnp.zeros((SUB, sz.E), F32)
        low = jnp.zeros((SUB, sz.E), F32)
        for k in range(sz.FR // SUB):
            row = (k // tiles) * sz.Q + (k % tiles) * SUB
            up = jnp.where(slot == k, lanes_of(u_ref[l, pl.ds(row + sz.Q - sz.face, SUB), :], last), up)
            low = jnp.where(slot == k, lanes_of(u_ref[l, pl.ds(row, SUB), :], first), low)
        halos.append((up, low))
    for j in range(sz.Z):
        at = 0
        for which, wanted in ((0, j in (0, 1)), (1, j in (0, sz.Z - 1))):
            if wanted:
                for l in range(sz.L):
                    zz[j][pl.ds(at, SUB), :] = halos[l][which]
                    at += SUB
        zz[j][pl.ds(at, sz.CH), :] = stage[lax.rem(z + j, sz.Z)]


def first_pack(sz, where, u):
    def body(where_ref, u_ref, *refs):
        pack(sz, where_ref, u_ref, refs[:-1], refs[-1])

    shapes = pack_shapes(sz)
    return call(body, shapes, [SMEM, VMEM], pack_scratch(sz), 0, 12 * sz.L * sz.R * sz.E)(where, u)


def inside(sz, in_hi, in_lo, u):
    pair = 2

    def body(hi_ref, lo_ref, u_ref, out_ref):
        for l in range(0, sz.L, pair):
            x = jnp.concatenate([u_ref[l + i] for i in range(pair)], axis=1)
            r = dot3(hi_ref[...], lo_ref[...], x)
            for i in range(pair):
                out_ref[l + i] = r[:, i * sz.E : (i + 1) * sz.E]

    out = jax.ShapeDtypeStruct(u.shape, F32)
    flops = 6 * sz.R * sz.R * sz.L * sz.E
    return call(body, [out], [VMEM] * 3, (), flops, 12 * u.size)(in_hi, in_lo, u)[0]


def turn_time(sz, where, parts):
    weights = [float(w) for w in time_weights(sz.T)]
    T, L, M = sz.T, sz.L, sz.M

    def body(where_ref, *refs):
        ins, outs, x_ref, y_ref = refs[:M], refs[M : 2 * M], refs[-2], refs[-1]
        me = where_ref[0]
        for j in range(M):
            x_ref[pl.ds((me ^ j) * L, L)] = ins[j][...]

        def rows(i, carry):
            at = pl.ds(pl.multiple_of(i * SUB, SUB), SUB)
            x = [x_ref[t, at, :] for t in range(T)]
            diff = {}
            for t in range(T):
                for k in range(1, T // 2):
                    a, b = (t + k) % T, (t - k) % T
                    if (b, a) not in diff:
                        diff[(a, b)] = x[a] - x[b]
            for t in range(T):
                total = None
                for k in range(1, T // 2):
                    a, b = (t + k) % T, (t - k) % T
                    term = weights[k] * diff[(a, b)] if (a, b) in diff else -weights[k] * diff[(b, a)]
                    total = term if total is None else total + term
                y_ref[t, at, :] = total
            return carry

        lax.fori_loop(0, sz.RC // SUB, rows, 0)
        for j in range(M):
            outs[j][...] = y_ref[pl.ds((me ^ j) * L, L)]

    shape = jax.ShapeDtypeStruct((L, sz.RC, sz.E), F32)
    full = pltpu.VMEM((T, sz.RC, sz.E), F32)
    size = T * sz.RC * sz.E
    return call(body, [shape] * M, [SMEM] + [VMEM] * M, [full, full], 20 * size, 8 * size)(where, *parts)


def shift_slide(sz, where, mine, theirs):
    Z, N, CH, E = sz.Z, sz.N, sz.CH, sz.E

    def body(where_ref, *refs):
        a, b, outs, x_ref = refs[:Z], refs[Z : 2 * Z], refs[2 * Z : 3 * Z], refs[-1]
        z, core = where_ref[1], where_ref[2]
        l = z // sz.PL
        group, shift = where_ref[3 + l], where_ref[3 + sz.L + l]
        for j in range(Z):
            chip = lax.rem(z + Z - j, Z)
            skip = sz.z_rows(j) - CH
            x_ref[2 * chip + core] = a[j][pl.ds(skip, CH), :]
            x_ref[2 * chip + 1 - core] = b[j][pl.ds(skip, CH), :]
        lane = iota((CH, E), 1)
        index = (lane + shift) % E
        for j in range(Z):
            block = 2 * lax.rem(z + j, Z) + core
            near = x_ref[lax.rem(block + group, N)]
            far = x_ref[lax.rem(block + group + 1, N)]
            outs[j][...] = lanes_of(jnp.where(lane < shift, far, near), index)

    out = jax.ShapeDtypeStruct((CH, E), F32)
    ins = [SMEM] + [VMEM] * (2 * Z)
    scratch = [pltpu.VMEM((N, CH, E), F32)]
    return call(body, [out] * Z, ins, scratch, 0, 12 * N * CH * E)(where, *mine, *theirs)


def finish(sz, last, where, angle, gaps, out_hi, out_lo, u, ins_part, times, slides, own, sibling, ahead, behind):
    L, E, R, FR, Q, face = sz.L, sz.E, sz.R, sz.FR, sz.Q, sz.face
    n_next = 0 if last else sz.M + sz.Z

    def body(where_ref, angle_ref, gaps_ref, hi_ref, lo_ref, u_ref, w_ref, *refs):
        time_refs, refs = refs[: sz.M], refs[sz.M :]
        slide_refs, refs = refs[: sz.Z], refs[sz.Z :]
        own_ref, sib_ref, ahead_ref, behind_ref = refs[:4]
        refs = refs[4:]
        new_ref, refs = refs[0], refs[1:]
        if last:
            res_ref, refs = refs[0], refs[1:]
        packs, refs = refs[:n_next], refs[n_next:]
        t_ref, s_ref, x_ref = refs[:3]
        me, z, core = where_ref[0], where_ref[1], where_ref[2]
        for j in range(sz.M):
            t_ref[:, pl.ds(pl.multiple_of((me ^ j) * sz.RC, SUB), sz.RC), :] = time_refs[j][...]
        for j in range(sz.Z):
            s_ref[lax.rem(z + sz.Z - j, sz.Z)] = slide_refs[j][...]
        lane = iota((SUB, E), 1)
        back = jnp.broadcast_to(gaps_ref[0:1, :], (SUB, E))
        front = jnp.broadcast_to(gaps_ref[1:2, :], (SUB, E))
        own_back = (lane + E - back) % E
        own_front = (lane + front) % E
        from_back = lane < back
        from_front = lane >= E - front
        first_core = core == 0
        tiles = face // SUB
        for l in range(L):
            prev_halo = jnp.where(first_core, behind_ref[pl.ds(l * SUB, SUB), :], sib_ref[pl.ds(l * SUB, SUB), :])
            next_halo = jnp.where(
                first_core, sib_ref[pl.ds(sz.H + l * SUB, SUB), :], ahead_ref[pl.ds(l * SUB, SUB), :]
            )
            for k in range(FR // SUB):
                row = (k // tiles) * Q + (k % tiles) * SUB
                here = lanes_of(u_ref[l, pl.ds(row + Q - face, SUB), :], own_back)
                there = lanes_of(prev_halo, (REACH * k + REACH + lane + E - back) % E)
                x_ref[pl.ds(k * SUB, SUB), pl.ds(l * E, E)] = jnp.where(from_back, there, here)
                here = lanes_of(u_ref[l, pl.ds(row, SUB), :], own_front)
                there = lanes_of(next_halo, (REACH * k + lane + front) % E)
                x_ref[pl.ds(FR + k * SUB, SUB), pl.ds(l * E, E)] = jnp.where(from_front, there, here)
            slide = [s_ref[l * sz.PL + i] for i in range(sz.PL)]
            slide = slide[0] if sz.PL == 1 else jnp.concatenate(slide, axis=0)
            x_ref[pl.ds(2 * FR, FR), pl.ds(l * E, E)] = slide
            v1 = slide[face : 2 * face]
            v2 = slide[2 * face : 3 * face]
            cosine, sine = angle_ref[0, l], angle_ref[1, l]
            x_ref[pl.ds(2 * FR + face, face), pl.ds(l * E, E)] = cosine * v1 - sine * v2
            x_ref[pl.ds(2 * FR + 2 * face, face), pl.ds(l * E, E)] = sine * v1 + cosine * v2
        pair = 2
        for l in range(0, L, pair):
            outer = dot3(hi_ref[...], lo_ref[...], x_ref[:, pl.ds(l * E, pair * E)])
            for i in range(pair):
                r = outer[:, i * E : (i + 1) * E] + w_ref[l + i] + t_ref[l + i]
                new_ref[l + i] = u_ref[l + i] - STEP * r
                if last:
                    res_ref[l + i] = r
        if not last:
            pack(sz, where_ref, new_ref, packs, refs[3])

    outs = [jax.ShapeDtypeStruct(u.shape, F32)]
    outs += [jax.ShapeDtypeStruct(u.shape, F32)] if last else pack_shapes(sz)
    scratch = [
        pltpu.VMEM((L, R, E), F32),
        pltpu.VMEM((sz.Z, sz.CH, E), F32),
        pltpu.VMEM((3 * FR, L * E), F32),
    ]
    if not last:
        scratch += pack_scratch(sz)
    ins = [SMEM, SMEM] + [VMEM] * (5 + sz.M + sz.Z + 4)
    args = (where, angle, gaps, out_hi, out_lo, u, ins_part, *times, *slides, own, sibling, ahead, behind)
    return call(body, outs, ins, scratch, 6 * R * 3 * FR * L * E, 24 * u.size)(*args)


def over_tm(x, j):
    size = lax.axis_size("tm")
    return lax.ppermute(x, "tm", [(i, i ^ j) for i in range(size)])


def over_chips(x, j):
    size = lax.axis_size("space")
    return lax.ppermute(x, "space", [(i, (i + 2 * j) % size) for i in range(size)])


def over_cores(x):
    size = lax.axis_size("space")
    return lax.ppermute(x, "space", [(i, i ^ 1) for i in range(size)])


def per_device(conserved_field, face_neighbours, counterpart_group, counterpart_shift, volume_operator, flux_matrix):
    sz = Sizes(conserved_field.shape)
    me = lax.axis_index("tm")
    s = lax.axis_index("space")
    where = jnp.concatenate([jnp.stack([me, s // 2, s % 2]), counterpart_group, counterpart_shift]).astype(jnp.int32)
    cycle = me * sz.L + jnp.arange(sz.L, dtype=jnp.int32)
    azimuth = 2.0 * jnp.pi * cycle.astype(F32) / sz.T
    angle = jnp.stack([jnp.cos(azimuth), jnp.sin(azimuth)])
    index = s * sz.E + jnp.arange(sz.E, dtype=jnp.int32)
    total = sz.E * sz.N
    gaps = jnp.stack([(index - face_neighbours[0]) % total, (face_neighbours[1] - index) % total])
    u = conserved_field.reshape(sz.L, sz.R, sz.E)
    in_hi, in_lo, out_hi, out_lo = matrices(sz, flux_matrix, volume_operator)
    packed = first_pack(sz, where, u)
    for sweep in range(ITERS):
        last = sweep == ITERS - 1
        tm, zz = packed[: sz.M], packed[sz.M :]
        parts = [tm[0]] + [over_tm(tm[j], j) for j in range(1, sz.M)]
        mine = [zz[0]] + [over_chips(zz[j], j) for j in range(1, sz.Z)]
        theirs = [over_cores(x) for x in mine]
        ins_part = inside(sz, in_hi, in_lo, u)
        times = turn_time(sz, where, parts)
        times = [times[0]] + [over_tm(times[j], j) for j in range(1, sz.M)]
        slides = shift_slide(sz, where, mine, theirs)
        slides = [slides[0]] + [over_chips(slides[j], j) for j in range(1, sz.Z)]
        done = finish(
            sz, last, where, angle, gaps, out_hi, out_lo, u, ins_part, times, slides,
            mine[0], theirs[0], theirs[sz.Z - 1], theirs[1],
        )
        u, packed = done[0], done[1:]
    shape = conserved_field.shape
    return u.reshape(shape), packed[0].reshape(shape)


def solution(mesh):
    return jax.shard_map(
        per_device,
        mesh=mesh,
        in_specs=(P("tm", None, None, "space"), P(None, "space"), P("tm"), P("tm"), P(), P()),
        out_specs=(P("tm", None, None, "space"), P("tm", None, None, "space")),
        check_vma=False,
    )
```

```python
import functools

import jax
import jax.numpy as jnp
import numpy as np
from jax import lax
from jax.experimental import pallas as pl
from jax.experimental.pallas import tpu as pltpu
from jax.sharding import PartitionSpec as P

REACH = 4
LIFT = 2.0
DISSIPATION = 1.5
ANGULAR = 0.5
DAMPING = 4.0
STEP = 0.2
SUB = 8

VMEM = pl.BlockSpec(memory_space=pltpu.VMEM)
SMEM = pl.BlockSpec(memory_space=pltpu.SMEM)
F32 = jnp.float32
BF16 = jnp.bfloat16


class Sizes:
    def __init__(self, field_shape):
        self.L, self.V, self.Q, self.E = field_shape
        self.R = self.V * self.Q
        self.M = lax.axis_size("tm")
        self.N = lax.axis_size("space")
        self.T = self.L * self.M
        self.Z = self.N // 2
        self.RC = self.R // self.M
        self.face = self.Q // 4
        self.FR = self.V * self.face
        self.PL = self.Z // self.L
        self.CH = self.FR // self.PL
        self.H = SUB * self.L

    def z_rows(self, j):
        if j == 0:
            return 2 * self.H + self.CH
        return self.CH + self.H * ((j == 1) + (j == self.Z - 1))


def time_weights(total):
    k = np.arange(1, total // 2, dtype=np.float64)
    gains = 2.0 * ANGULAR * k * np.exp(-DAMPING * (k / (total // 2)) ** 8) / total
    lag = np.arange(total, dtype=np.float64)
    return np.sum(gains[:, None] * np.sin(2.0 * np.pi * k[:, None] * lag[None, :] / total), axis=0)


def call(body, outs, ins, scratch=(), flops=0, nbytes=0):
    return pl.pallas_call(
        body,
        out_shape=outs,
        in_specs=ins,
        out_specs=jax.tree.map(lambda _: VMEM, outs),
        scratch_shapes=list(scratch),
        cost_estimate=pl.CostEstimate(flops=flops, bytes_accessed=nbytes, transcendentals=0),
        compiler_params=pltpu.CompilerParams(vmem_limit_bytes=16 * 1024 * 1024),
    )


def spot():
    s = lax.axis_index("space")
    return lax.axis_index("tm"), s // 2, lax.rem(s, 2)


def turn_of(sz, l):
    me = lax.axis_index("tm")
    cosine, sine = jnp.float32(1.0), jnp.float32(0.0)
    for m in range(sz.M):
        azimuth = 2.0 * np.pi * (m * sz.L + l) / sz.T
        cosine = jnp.where(me == m, jnp.float32(np.cos(azimuth)), cosine)
        sine = jnp.where(me == m, jnp.float32(np.sin(azimuth)), sine)
    return cosine, sine


def lanes_of(x, index):
    return jnp.take_along_axis(x, index, axis=1, mode="promise_in_bounds")


def split(x):
    hi = x.astype(BF16)
    return hi, (x - hi.astype(F32)).astype(BF16)


def dot3(a_hi, a_lo, x):
    x_hi, x_lo = split(x)
    out = jnp.dot(a_hi, x_hi, preferred_element_type=F32)
    out += jnp.dot(a_hi, x_lo, preferred_element_type=F32)
    return out + jnp.dot(a_lo, x_hi, preferred_element_type=F32)


def iota(shape, axis):
    return lax.broadcasted_iota(jnp.int32, shape, axis)


def matrices(sz, flux, volume_operator):
    V, Q, face = sz.V, sz.Q, sz.face

    def body(flux_ref, vol_ref, in_hi, in_lo, out_hi, out_lo):
        p = iota((Q, Q), 0)
        q = iota((Q, Q), 1)
        same = p == q
        low = same & (p < face)
        up = same & (p >= Q - face)
        slide = same & (p % 4 == 3)
        fp = iota((Q, face), 0)
        fq = iota((Q, face), 1)
        to_low = fp == fq
        to_up = fp == fq + (Q - face)
        to_slide = fp == 4 * fq + 3
        vol0 = vol_ref[0]
        vol1 = vol_ref[1]
        for v in range(V):
            blocks = []
            lows, ups, slides = [], [], []
            for w in range(V):
                f0 = flux_ref[0, v, w]
                f1 = flux_ref[1, v, w]
                d = DISSIPATION if v == w else 0.0
                a_low = 0.5 * LIFT * (-f0 - d)
                a_up = 0.5 * LIFT * (f0 - d)
                a_slide = 0.5 * LIFT * (f1 - d)
                block = f0 * vol0 + f1 * vol1
                block -= jnp.where(low, a_low, 0.0)
                block -= jnp.where(up, a_up, 0.0)
                block -= jnp.where(slide, a_slide, 0.0)
                blocks.append(block)
                lows.append(jnp.where(to_low, a_low, 0.0))
                ups.append(jnp.where(to_up, a_up, 0.0))
                slides.append(jnp.where(to_slide, a_slide, 0.0))
            hi, lo = split(jnp.concatenate(blocks, axis=1))
            in_hi[pl.ds(v * Q, Q), :] = hi
            in_lo[pl.ds(v * Q, Q), :] = lo
            hi, lo = split(jnp.concatenate(lows + ups + slides, axis=1))
            out_hi[pl.ds(v * Q, Q), :] = hi
            out_lo[pl.ds(v * Q, Q), :] = lo

    inner = jax.ShapeDtypeStruct((sz.R, sz.R), BF16)
    outer = jax.ShapeDtypeStruct((sz.R, 3 * sz.FR), BF16)
    nbytes = 4 * sz.R * (sz.R + 3 * sz.FR)
    return call(body, [inner, inner, outer, outer], [SMEM, VMEM], (), nbytes, nbytes)(flux, volume_operator)


def tm_shapes(sz, rows):
    return [jax.ShapeDtypeStruct((sz.L, rows, sz.E), F32) for _ in range(sz.M)]


def chip_shapes(sz):
    return [jax.ShapeDtypeStruct((sz.z_rows(j), sz.E), F32) for j in range(sz.Z)]


def pack_time(sz, u):
    def body(u_ref, *refs):
        outs, sems = refs[: sz.M], refs[-1]
        me = lax.axis_index("tm")
        copies = []
        for j in list(range(1, sz.M)) + [0]:
            start = pl.multiple_of((me ^ j) * sz.RC, SUB)
            copies.append(pltpu.make_async_copy(u_ref.at[:, pl.ds(start, sz.RC), :], outs[j], sems.at[j]))
            copies[-1].start()
        for copy in copies:
            copy.wait()

    scratch = [pltpu.SemaphoreType.DMA((sz.M,))]
    source = pl.BlockSpec(memory_space=pltpu.HBM)
    return call(body, tm_shapes(sz, sz.RC), [source], scratch, 0, 8 * u.size)(u)


def chip_scratch(sz):
    return pltpu.VMEM((sz.Z, sz.CH, sz.E), F32)


def pack_chips(sz, slide_ref, halo_ref, zz, stage):
    z = spot()[1]
    for p in range(sz.Z):
        first = (p % sz.PL) * sz.CH
        stage[p] = slide_ref[p // sz.PL, pl.ds(3 + 4 * first, sz.CH, stride=4), :]
    lane = iota((SUB, sz.E), 1)
    slot = lane // REACH
    last = sz.E - REACH + lane % REACH
    first = lane % REACH
    tiles = sz.face // SUB
    halos = []
    for l in range(sz.L):
        up = jnp.zeros((SUB, sz.E), F32)
        low = jnp.zeros((SUB, sz.E), F32)
        for k in range(sz.FR // SUB):
            row = (k // tiles) * sz.Q + (k % tiles) * SUB
            up = jnp.where(slot == k, lanes_of(halo_ref[l, pl.ds(row + sz.Q - sz.face, SUB), :], last), up)
            low = jnp.where(slot == k, lanes_of(halo_ref[l, pl.ds(row, SUB), :], first), low)
        halos.append((up, low))
    for j in range(sz.Z):
        at = 0
        for which, wanted in ((0, j in (0, 1)), (1, j in (0, sz.Z - 1))):
            if wanted:
                for l in range(sz.L):
                    zz[j][pl.ds(at, SUB), :] = halos[l][which]
                    at += SUB
        zz[j][pl.ds(at, sz.CH), :] = stage[lax.rem(z + j, sz.Z)]


def pack_space(sz, u):
    def body(u_ref, *refs):
        held, sem = refs[-2], refs[-1]
        copy = pltpu.make_async_copy(u_ref, held, sem)
        copy.start()
        copy.wait()
        pack_chips(sz, held, held, refs[:-3], refs[-3])

    scratch = [chip_scratch(sz), pltpu.VMEM(u.shape, F32), pltpu.SemaphoreType.DMA]
    source = pl.BlockSpec(memory_space=pltpu.HBM)
    return call(body, chip_shapes(sz), [source], scratch, 0, 4 * u.size)(u)


def inside_part(sz, mats, u):
    E, pair = sz.E, 2

    def body(hi_ref, lo_ref, u_ref, out_ref):
        for l in range(0, sz.L, pair):
            x = jnp.concatenate([u_ref[l + i] for i in range(pair)], axis=1)
            r = dot3(hi_ref[...], lo_ref[...], x)
            for i in range(pair):
                out_ref[l + i] = r[:, i * E : (i + 1) * E]

    out = jax.ShapeDtypeStruct(u.shape, F32)
    return call(body, [out], [VMEM] * 3, (), 6 * sz.R * u.size, 12 * u.size)(*mats[:2], u)[0]


def face_part(sz, neighbours, mats, u, inner, own, sibling, ahead, behind):
    L, E, FR, Q, face = sz.L, sz.E, sz.FR, sz.Q, sz.face
    pair = 2

    def body(near_ref, ohi_ref, olo_ref, u_ref, in_ref, sib_ref, ahead_ref, behind_ref, out_ref, x_ref):
        core = spot()[2]
        lane = iota((SUB, E), 1)
        index = lax.axis_index("space") * E + lane
        total = sz.N * E
        back = index - jnp.broadcast_to(near_ref[0:1, :], (SUB, E))
        back = jnp.where(back < 0, back + total, back)
        front = jnp.broadcast_to(near_ref[1:2, :], (SUB, E)) - index
        front = jnp.where(front < 0, front + total, front)
        own_back = (lane + E - back) % E
        own_front = (lane + front) % E
        from_back = lane < back
        from_front = lane >= E - front
        first_core = core == 0
        tiles = face // SUB
        for l in range(L):
            prev_halo = jnp.where(first_core, behind_ref[pl.ds(l * SUB, SUB), :], sib_ref[pl.ds(l * SUB, SUB), :])
            next_halo = jnp.where(
                first_core, sib_ref[pl.ds(sz.H + l * SUB, SUB), :], ahead_ref[pl.ds(l * SUB, SUB), :]
            )
            for k in range(FR // SUB):
                row = (k // tiles) * Q + (k % tiles) * SUB
                here = lanes_of(u_ref[l, pl.ds(row + Q - face, SUB), :], own_back)
                there = lanes_of(prev_halo, (REACH * k + REACH + lane + E - back) % E)
                x_ref[pl.ds(k * SUB, SUB), pl.ds(l * E, E)] = jnp.where(from_back, there, here)
                here = lanes_of(u_ref[l, pl.ds(row, SUB), :], own_front)
                there = lanes_of(next_halo, (REACH * k + lane + front) % E)
                x_ref[pl.ds(FR + k * SUB, SUB), pl.ds(l * E, E)] = jnp.where(from_front, there, here)
        for l in range(0, L, pair):
            x = x_ref[:, pl.ds(l * E, pair * E)]
            r = dot3(ohi_ref[:, : 2 * FR], olo_ref[:, : 2 * FR], x)
            for i in range(pair):
                out_ref[l + i] = in_ref[l + i] + r[:, i * E : (i + 1) * E]

    out = jax.ShapeDtypeStruct(u.shape, F32)
    flops = 12 * sz.R * FR * L * E
    ins = [VMEM] * 8
    scratch = [pltpu.VMEM((2 * FR, L * E), F32)]
    args = (neighbours, *mats[2:], u, inner, sibling, ahead, behind)
    return call(body, [out], ins, scratch, flops, 12 * u.size)(*args)[0]


def turn_time(sz, parts, damp=False, carried=()):
    weights = [float(w) for w in time_weights(sz.T)]
    T, L, M = sz.T, sz.L, sz.M
    rows = parts[0].shape[1]
    padded = -(-rows // SUB) * SUB
    front = carried[0].shape[1] if carried else 0

    def body(*refs):
        ins, fronts, outs, x_ref, y_ref = refs[:M], refs[M : M + len(carried)], refs[-2 - M : -2], refs[-2], refs[-1]
        me = spot()[0]
        for j in range(len(carried)):
            outs[j][:, pl.ds(0, front), :] = fronts[j][...]
        for j in range(M):
            x_ref[pl.ds((me ^ j) * L, L), pl.ds(0, rows), :] = ins[j][...]

        def some(i, carry):
            at = pl.ds(pl.multiple_of(i * SUB, SUB), SUB)
            x = [x_ref[t, at, :] for t in range(T)]
            diff = {}
            for t in range(T):
                total = None
                for k in range(1, T // 2):
                    a, b = (t + k) % T, (t - k) % T
                    if (a, b) not in diff and (b, a) not in diff:
                        diff[(a, b)] = x[a] - x[b]
                    term = weights[k] * diff[(a, b)] if (a, b) in diff else -weights[k] * diff[(b, a)]
                    total = term if total is None else total + term
                y_ref[t, at, :] = x[t] - STEP * total if damp else total
            return carry

        lax.fori_loop(0, padded // SUB, some, 0)
        for j in range(M):
            outs[j][:, pl.ds(front, rows), :] = y_ref[pl.ds((me ^ j) * L, L), pl.ds(0, rows), :]

    full = pltpu.VMEM((T, padded, sz.E), F32)
    size = T * rows * sz.E
    ins = [VMEM] * (M + len(carried))
    shapes = tm_shapes(sz, front + rows)
    return call(body, shapes, ins, [full, full], 20 * size, 8 * size)(*parts, *carried)


def shift_slide(sz, groups, shifts, mine, theirs):
    Z, N, CH, E = sz.Z, sz.N, sz.CH, sz.E

    def body(group_ref, shift_ref, *refs):
        a, b, outs, x_ref = refs[:Z], refs[Z : 2 * Z], refs[2 * Z : 3 * Z], refs[-1]
        _, z, core = spot()
        l = z // sz.PL
        group, shift = group_ref[l], shift_ref[l]
        for j in range(Z):
            chip = lax.rem(z + Z - j, Z)
            skip = sz.z_rows(j) - CH
            x_ref[2 * chip + core] = a[j][pl.ds(skip, CH), :]
            x_ref[2 * chip + 1 - core] = b[j][pl.ds(skip, CH), :]
        lane = iota((CH, E), 1)
        index = (lane + shift) % E
        for j in range(Z):
            block = 2 * lax.rem(z + j, Z) + core
            near = x_ref[lax.rem(block + group, N)]
            far = x_ref[lax.rem(block + group + 1, N)]
            outs[j][...] = lanes_of(jnp.where(lane < shift, far, near), index)

    out = jax.ShapeDtypeStruct((CH, E), F32)
    ins = [SMEM, SMEM] + [VMEM] * (2 * Z)
    scratch = [pltpu.VMEM((N, CH, E), F32)]
    return call(body, [out] * Z, ins, scratch, 0, 12 * N * CH * E)(groups, shifts, *mine, *theirs)


def slide_rows(sz, slides, stage, x_ref):
    E, face, FR = sz.E, sz.face, sz.FR
    z = spot()[1]
    for j in range(sz.Z):
        stage[lax.rem(z + sz.Z - j, sz.Z)] = slides[j][...]
    for l in range(sz.L):
        slide = [stage[l * sz.PL + i] for i in range(sz.PL)]
        slide = slide[0] if sz.PL == 1 else jnp.concatenate(slide, axis=0)
        cols = pl.ds(l * E, E)
        x_ref[:, cols] = slide
        v1 = slide[face : 2 * face]
        v2 = slide[2 * face : 3 * face]
        cosine, sine = turn_of(sz, l)
        x_ref[pl.ds(face, face), cols] = cosine * v1 - sine * v2
        x_ref[pl.ds(2 * face, face), cols] = sine * v1 + cosine * v2


def gather_rows(sz, parts, full):
    me = spot()[0]
    for j in range(sz.M):
        full[:, pl.ds(pl.multiple_of((me ^ j) * sz.RC, SUB), sz.RC), :] = parts[j][...]


def first_slide(sz, mats, u, local, slides):
    L, E, R, FR, M = sz.L, sz.E, sz.R, sz.FR, sz.M
    CR = FR // M
    pair = 2

    def body(ohi_ref, olo_ref, u_ref, w_ref, *refs):
        slide_refs, out_ref, chunks = refs[: sz.Z], refs[sz.Z], refs[sz.Z + 1 : sz.Z + 1 + M]
        stage, x_ref, cut_ref = refs[-3:]
        slide_rows(sz, slide_refs, stage, x_ref)
        for l in range(L):
            for m in range(M):
                cut_ref[m, l] = x_ref[pl.ds(m * CR, CR), pl.ds(l * E, E)]
        for j in range(M):
            chunks[j][...] = cut_ref[spot()[0] ^ j]
        for l in range(0, L, pair):
            outer = dot3(ohi_ref[:, 2 * FR :], olo_ref[:, 2 * FR :], x_ref[:, pl.ds(l * E, pair * E)])
            for i in range(pair):
                out_ref[l + i] = u_ref[l + i] - STEP * (w_ref[l + i] + outer[:, i * E : (i + 1) * E])

    outs = [jax.ShapeDtypeStruct(u.shape, F32)] + tm_shapes(sz, CR)
    scratch = [chip_scratch(sz), pltpu.VMEM((FR, L * E), F32), pltpu.VMEM((M, L, CR, E), F32)]
    ins = [VMEM] * (4 + sz.Z)
    done = call(body, outs, ins, scratch, 6 * R * FR * L * E, 12 * u.size)(*mats[2:], u, local, *slides)
    return done[0], done[1:]


def first_step(sz, partial, times):
    def body(c_ref, *refs):
        time_refs, u_ref, v_ref = refs[: sz.M], refs[sz.M], refs[sz.M + 1]
        zz, t_ref, stage = refs[sz.M + 2 : -2], refs[-2], refs[-1]
        gather_rows(sz, time_refs, t_ref)
        for l in range(sz.L):
            t = STEP * t_ref[l]
            new = c_ref[l] - t
            u_ref[l] = new
            v_ref[l] = new - t
        pack_chips(sz, u_ref, v_ref, zz, stage)

    full = jax.ShapeDtypeStruct(partial.shape, F32)
    scratch = [pltpu.VMEM(partial.shape, F32), chip_scratch(sz)]
    ins = [VMEM] * (1 + sz.M)
    done = call(body, [full, full] + chip_shapes(sz), ins, scratch, 0, 16 * partial.size)(partial, *times)
    return done[0], done[1], done[2:]


def last_step(sz, mats, u, local, times, slides):
    L, E, R, FR, M = sz.L, sz.E, sz.R, sz.FR, sz.M
    CR = FR // M
    pair = 2

    def body(ohi_ref, olo_ref, u_ref, w_ref, *refs):
        time_refs, refs = refs[:M], refs[M:]
        slide_refs, refs = refs[: sz.Z], refs[sz.Z :]
        new_ref, res_ref, t_ref, stage, x_ref, cut_ref = refs
        me = spot()[0]
        for j in range(M):
            t_ref[me ^ j] = time_refs[j][:, pl.ds(0, sz.RC), :]
            cut_ref[me ^ j] = time_refs[j][:, pl.ds(sz.RC, CR), :]
        slide_rows(sz, slide_refs, stage, x_ref)
        for l in range(L):
            for m in range(M):
                x_ref[pl.ds(m * CR, CR), pl.ds(l * E, E)] -= STEP * cut_ref[m, l]
        for l in range(0, L, pair):
            outer = dot3(ohi_ref[:, 2 * FR :], olo_ref[:, 2 * FR :], x_ref[:, pl.ds(l * E, pair * E)])
            for i in range(pair):
                for m in range(M):
                    rows = slice(m * sz.RC, (m + 1) * sz.RC)
                    r = outer[rows, i * E : (i + 1) * E] + w_ref[l + i, rows] + t_ref[m, l + i]
                    new_ref[l + i, rows] = u_ref[l + i, rows] - STEP * r
                    res_ref[l + i, rows] = r

    full = jax.ShapeDtypeStruct(u.shape, F32)
    scratch = [pltpu.VMEM((M, L, sz.RC, E), F32)]
    scratch += [chip_scratch(sz), pltpu.VMEM((FR, L * E), F32), pltpu.VMEM((M, L, CR, E), F32)]
    ins = [VMEM] * (4 + M + sz.Z)
    args = (*mats[2:], u, local, *times, *slides)
    return call(body, [full, full], ins, scratch, 6 * R * FR * L * E, 20 * u.size)(*args)


def over_tm(x, j):
    size = lax.axis_size("tm")
    return lax.ppermute(x, "tm", [(i, i ^ j) for i in range(size)])


def over_chips(x, j):
    size = lax.axis_size("space")
    return lax.ppermute(x, "space", [(i, (i + 2 * j) % size) for i in range(size)])


def over_cores(x):
    size = lax.axis_size("space")
    return lax.ppermute(x, "space", [(i, i ^ 1) for i in range(size)])


def per_device(conserved_field, face_neighbours, counterpart_group, counterpart_shift, volume_operator, flux_matrix):
    sz = Sizes(conserved_field.shape)
    u = conserved_field.reshape(sz.L, sz.R, sz.E)

    def time_trip(parts):
        return [parts[0]] + [over_tm(parts[j], j) for j in range(1, sz.M)]

    def chip_trip(parts):
        return [parts[0]] + [over_chips(parts[j], j) for j in range(1, sz.Z)]

    def faces(field, inner, mine, theirs):
        return face_part(sz, face_neighbours, mats, field, inner, mine[0], theirs[0], theirs[sz.Z - 1], theirs[1])

    chunks = pack_time(sz, u)
    parts = time_trip(chunks)
    packed = pack_space(sz, after(u, chunks[0]))
    mats = matrices(sz, after(flux_matrix, packed[0]), volume_operator)
    packed = [*packed[:-1], after(packed[-1], mats[0])]
    mine = chip_trip(packed)
    inner = inside_part(sz, mats, u)
    turned = turn_time(sz, after(parts, inner))
    times = time_trip(turned)
    theirs = [over_cores(x) for x in mine[:1] + after(mine[1:], turned[0])]
    shifted = shift_slide(sz, counterpart_group, counterpart_shift, mine, theirs)
    slides = chip_trip(shifted)
    here = faces(after(u, shifted[0]), inner, mine, theirs)
    damped = turn_time(sz, after(turned, here), damp=True)
    partial, cuts = first_slide(sz, mats, u, after(here, damped), slides)
    cut_parts = time_trip(cuts)
    u, v, packed = first_step(sz, partial, times)
    mine = chip_trip(packed)
    inner = inside_part(sz, mats, v)
    both = turn_time(sz, after(cut_parts, inner), carried=damped)
    times = time_trip(both)
    theirs = [over_cores(x) for x in mine[:1] + after(mine[1:], both[0])]
    shifted = shift_slide(sz, counterpart_group, counterpart_shift, mine, theirs)
    slides = chip_trip(shifted)
    here = faces(after(v, shifted[0]), inner, mine, theirs)
    new, residual = last_step(sz, mats, u, here, times, slides)
    shape = conserved_field.shape
    return new.reshape(shape), residual.reshape(shape)


def after(values, anchor):
    return lax.optimization_barrier((values, anchor))[0]


def solution(mesh):
    return jax.shard_map(
        per_device,
        mesh=mesh,
        in_specs=(P("tm", None, None, "space"), P(None, "space"), P("tm"), P("tm"), P(), P()),
        out_specs=(P("tm", None, None, "space"), P("tm", None, None, "space")),
        check_vma=False,
    )
```

```python
import functools

import jax
import jax.numpy as jnp
import numpy as np
from jax import lax
from jax.experimental import pallas as pl
from jax.experimental.pallas import tpu as pltpu
from jax.sharding import PartitionSpec as P

REACH = 4
LIFT = 2.0
DISSIPATION = 1.5
ANGULAR = 0.5
DAMPING = 4.0
STEP = 0.2
SUB = 8

VMEM = pl.BlockSpec(memory_space=pltpu.VMEM)
SMEM = pl.BlockSpec(memory_space=pltpu.SMEM)
F32 = jnp.float32
BF16 = jnp.bfloat16


class Sizes:
    def __init__(self, field_shape):
        self.L, self.V, self.Q, self.E = field_shape
        self.R = self.V * self.Q
        self.M = lax.axis_size("tm")
        self.N = lax.axis_size("space")
        self.T = self.L * self.M
        self.Z = self.N // 2
        self.half = self.Z // 2
        self.RC = self.R // self.M
        self.face = self.Q // 4
        self.FR = self.V * self.face
        self.PL = self.Z // self.L
        self.CH = self.FR // self.PL
        self.H = SUB * self.L

    def z_rows(self, j):
        if j == 0:
            return 2 * self.H + self.CH
        return self.CH + self.H * ((j == 1) + (j == self.Z - 1))

    def front(self, j):
        return self.H if j == 1 else 0

    def ahead(self, z, core, j):
        return lax.rem(z + self.Z + jnp.where(core == 0, j, -j), self.Z)


def time_weights(total):
    k = np.arange(1, total // 2, dtype=np.float64)
    gains = 2.0 * ANGULAR * k * np.exp(-DAMPING * (k / (total // 2)) ** 8) / total
    lag = np.arange(total, dtype=np.float64)
    return np.sum(gains[:, None] * np.sin(2.0 * np.pi * k[:, None] * lag[None, :] / total), axis=0)


def call(body, outs, ins, scratch=(), flops=0, nbytes=0):
    return pl.pallas_call(
        body,
        out_shape=outs,
        in_specs=ins,
        out_specs=jax.tree.map(lambda _: VMEM, outs),
        scratch_shapes=list(scratch),
        cost_estimate=pl.CostEstimate(flops=flops, bytes_accessed=nbytes, transcendentals=0),
        compiler_params=pltpu.CompilerParams(vmem_limit_bytes=16 * 1024 * 1024),
    )


def spot():
    s = lax.axis_index("space")
    return lax.axis_index("tm"), s // 2, lax.rem(s, 2)


def turn_of(sz, l):
    me = lax.axis_index("tm")
    cosine, sine = jnp.float32(1.0), jnp.float32(0.0)
    for m in range(sz.M):
        azimuth = 2.0 * np.pi * (m * sz.L + l) / sz.T
        cosine = jnp.where(me == m, jnp.float32(np.cos(azimuth)), cosine)
        sine = jnp.where(me == m, jnp.float32(np.sin(azimuth)), sine)
    return cosine, sine


def lanes_of(x, index):
    return jnp.take_along_axis(x, index, axis=1, mode="promise_in_bounds")


def split(x):
    hi = x.astype(BF16)
    return hi, (x - hi.astype(F32)).astype(BF16)


def dot3(a_hi, a_lo, x):
    x_hi, x_lo = split(x)
    out = jnp.dot(a_hi, x_hi, preferred_element_type=F32)
    out += jnp.dot(a_hi, x_lo, preferred_element_type=F32)
    return out + jnp.dot(a_lo, x_hi, preferred_element_type=F32)


def iota(shape, axis):
    return lax.broadcasted_iota(jnp.int32, shape, axis)


def matrices(sz, flux, volume_operator):
    V, Q, face = sz.V, sz.Q, sz.face

    def body(flux_ref, vol_ref, in_hi, in_lo, out_hi, out_lo):
        p = iota((Q, Q), 0)
        q = iota((Q, Q), 1)
        same = p == q
        low = same & (p < face)
        up = same & (p >= Q - face)
        slide = same & (p % 4 == 3)
        fp = iota((Q, face), 0)
        fq = iota((Q, face), 1)
        to_low = fp == fq
        to_up = fp == fq + (Q - face)
        to_slide = fp == 4 * fq + 3
        vol0 = vol_ref[0]
        vol1 = vol_ref[1]
        for v in range(V):
            blocks = []
            lows, ups, slides = [], [], []
            for w in range(V):
                f0 = flux_ref[0, v, w]
                f1 = flux_ref[1, v, w]
                d = DISSIPATION if v == w else 0.0
                a_low = 0.5 * LIFT * (-f0 - d)
                a_up = 0.5 * LIFT * (f0 - d)
                a_slide = 0.5 * LIFT * (f1 - d)
                block = f0 * vol0 + f1 * vol1
                block -= jnp.where(low, a_low, 0.0)
                block -= jnp.where(up, a_up, 0.0)
                block -= jnp.where(slide, a_slide, 0.0)
                blocks.append(block)
                lows.append(jnp.where(to_low, a_low, 0.0))
                ups.append(jnp.where(to_up, a_up, 0.0))
                slides.append(jnp.where(to_slide, a_slide, 0.0))
            hi, lo = split(jnp.concatenate(blocks, axis=1))
            in_hi[pl.ds(v * Q, Q), :] = hi
            in_lo[pl.ds(v * Q, Q), :] = lo
            hi, lo = split(jnp.concatenate(lows + ups + slides, axis=1))
            out_hi[pl.ds(v * Q, Q), :] = hi
            out_lo[pl.ds(v * Q, Q), :] = lo

    inner = jax.ShapeDtypeStruct((sz.R, sz.R), BF16)
    outer = jax.ShapeDtypeStruct((sz.R, 3 * sz.FR), BF16)
    nbytes = 4 * sz.R * (sz.R + 3 * sz.FR)
    return call(body, [inner, inner, outer, outer], [SMEM, VMEM], (), nbytes, nbytes)(flux, volume_operator)


def tm_shapes(sz, rows):
    return [jax.ShapeDtypeStruct((sz.L, rows, sz.E), F32) for _ in range(sz.M)]


def chip_shapes(sz):
    block = (sz.CH, sz.E)
    return [
        jax.ShapeDtypeStruct((sz.half + 2, *block), F32),
        jax.ShapeDtypeStruct((sz.half, *block), F32),
        jax.ShapeDtypeStruct(block, F32),
    ]


def pack_time(sz, u):
    def body(u_ref, *refs):
        outs, sems = refs[: sz.M], refs[-1]
        me = lax.axis_index("tm")
        copies = []
        for j in list(range(1, sz.M)) + [0]:
            start = pl.multiple_of((me ^ j) * sz.RC, SUB)
            copies.append(pltpu.make_async_copy(u_ref.at[:, pl.ds(start, sz.RC), :], outs[j], sems.at[j]))
            copies[-1].start()
        for copy in copies:
            copy.wait()

    scratch = [pltpu.SemaphoreType.DMA((sz.M,))]
    source = pl.BlockSpec(memory_space=pltpu.HBM)
    return call(body, tm_shapes(sz, sz.RC), [source], scratch, 0, 8 * u.size)(u)


def chip_scratch(sz):
    return pltpu.VMEM((sz.Z, sz.CH, sz.E), F32)


def pack_chips(sz, slide_ref, halo_ref, outs, stage):
    swap_ref, keep_ref, far_ref = outs
    _, z, core = spot()
    for p in range(sz.Z):
        first = (p % sz.PL) * sz.CH
        stage[p] = slide_ref[p // sz.PL, pl.ds(3 + 4 * first, sz.CH, stride=4), :]
    for j in range(sz.half):
        swap_ref[j] = stage[sz.ahead(z, 1 - core, j)]
        keep_ref[j] = stage[sz.ahead(z, core, j)]
    far_ref[...] = stage[lax.rem(z + sz.half, sz.Z)]
    lane = iota((SUB, sz.E), 1)
    slot = lane // REACH
    last = sz.E - REACH + lane % REACH
    first = lane % REACH
    tiles = sz.face // SUB
    for l in range(sz.L):
        up = jnp.zeros((SUB, sz.E), F32)
        low = jnp.zeros((SUB, sz.E), F32)
        for k in range(sz.FR // SUB):
            row = (k // tiles) * sz.Q + (k % tiles) * SUB
            up = jnp.where(slot == k, lanes_of(halo_ref[l, pl.ds(row + sz.Q - sz.face, SUB), :], last), up)
            low = jnp.where(slot == k, lanes_of(halo_ref[l, pl.ds(row, SUB), :], first), low)
        swap_ref[sz.half, pl.ds(l * SUB, SUB), :] = up
        swap_ref[sz.half + 1, pl.ds(l * SUB, SUB), :] = low


def ring_shapes(sz):
    return [jax.ShapeDtypeStruct((sz.z_rows(j), sz.E), F32) for j in range(sz.Z)]


def pack_ring(sz, slide_ref, halo_ref, zz, stage):
    z = spot()[1]
    for p in range(sz.Z):
        first = (p % sz.PL) * sz.CH
        stage[p] = slide_ref[p // sz.PL, pl.ds(3 + 4 * first, sz.CH, stride=4), :]
    lane = iota((SUB, sz.E), 1)
    slot = lane // REACH
    last = sz.E - REACH + lane % REACH
    first = lane % REACH
    tiles = sz.face // SUB
    halos = []
    for l in range(sz.L):
        up = jnp.zeros((SUB, sz.E), F32)
        low = jnp.zeros((SUB, sz.E), F32)
        for k in range(sz.FR // SUB):
            row = (k // tiles) * sz.Q + (k % tiles) * SUB
            up = jnp.where(slot == k, lanes_of(halo_ref[l, pl.ds(row + sz.Q - sz.face, SUB), :], last), up)
            low = jnp.where(slot == k, lanes_of(halo_ref[l, pl.ds(row, SUB), :], first), low)
        halos.append((up, low))
    for j in range(sz.Z):
        at = 0
        for which, wanted in ((0, j in (0, 1)), (1, j in (0, sz.Z - 1))):
            if wanted:
                for l in range(sz.L):
                    zz[j][pl.ds(at, SUB), :] = halos[l][which]
                    at += SUB
        zz[j][pl.ds(at, sz.CH), :] = stage[lax.rem(z + j, sz.Z)]


def shift_ring(sz, groups, shifts, mine, theirs):
    Z, N, CH, E = sz.Z, sz.N, sz.CH, sz.E

    def body(group_ref, shift_ref, *refs):
        a, b, outs, x_ref = refs[:Z], refs[Z : 2 * Z], refs[2 * Z : 3 * Z], refs[-1]
        _, z, core = spot()
        l = z // sz.PL
        group, shift = group_ref[l], shift_ref[l]
        for j in range(Z):
            chip = lax.rem(z + Z - j, Z)
            skip = sz.z_rows(j) - CH
            x_ref[2 * chip + core] = a[j][pl.ds(skip, CH), :]
            x_ref[2 * chip + 1 - core] = b[j][pl.ds(skip, CH), :]
        lane = iota((CH, E), 1)
        index = (lane + shift) % E
        for j in range(Z):
            block = 2 * lax.rem(z + j, Z) + core
            near = x_ref[lax.rem(block + group, N)]
            far = x_ref[lax.rem(block + group + 1, N)]
            outs[j][...] = lanes_of(jnp.where(lane < shift, far, near), index)

    out = jax.ShapeDtypeStruct((CH, E), F32)
    ins = [SMEM, SMEM] + [VMEM] * (2 * Z)
    scratch = [pltpu.VMEM((N, CH, E), F32)]
    return call(body, [out] * Z, ins, scratch, 0, 12 * N * CH * E)(groups, shifts, *mine, *theirs)


def join_cores(sz, keep, swapped):
    def body(keep_ref, swap_ref, *outs):
        core = spot()[2]
        for j in range(1, sz.half):
            out, front = outs[j - 1], sz.front(j)
            if front:
                out[pl.ds(0, front), :] = swap_ref[sz.half + core, pl.ds(0, front), :]
            out[pl.ds(front, sz.CH), :] = keep_ref[j]
            out[pl.ds(front + sz.CH, sz.CH), :] = swap_ref[j]

    shapes = [jax.ShapeDtypeStruct((sz.front(j) + 2 * sz.CH, sz.E), F32) for j in range(1, sz.half)]
    return call(body, shapes, [VMEM, VMEM], (), 0, 16 * sz.half * sz.CH * sz.E)(keep, swapped)


def pack_space(sz, u):
    def body(u_ref, *refs):
        held, sem = refs[-2], refs[-1]
        copy = pltpu.make_async_copy(u_ref, held, sem)
        copy.start()
        copy.wait()
        pack_chips(sz, held, held, refs[:-3], refs[-3])

    scratch = [chip_scratch(sz), pltpu.VMEM(u.shape, F32), pltpu.SemaphoreType.DMA]
    source = pl.BlockSpec(memory_space=pltpu.HBM)
    return call(body, chip_shapes(sz), [source], scratch, 0, 4 * u.size)(u)


def inside_part(sz, mats, u):
    E, pair = sz.E, 2

    def body(hi_ref, lo_ref, u_ref, out_ref):
        for l in range(0, sz.L, pair):
            x = jnp.concatenate([u_ref[l + i] for i in range(pair)], axis=1)
            r = dot3(hi_ref[...], lo_ref[...], x)
            for i in range(pair):
                out_ref[l + i] = r[:, i * E : (i + 1) * E]

    out = jax.ShapeDtypeStruct(u.shape, F32)
    return call(body, [out], [VMEM] * 3, (), 6 * sz.R * u.size, 12 * u.size)(*mats[:2], u)[0]


def face_part(sz, neighbours, mats, u, inner, *halos):
    L, E, FR, Q, face = sz.L, sz.E, sz.FR, sz.Q, sz.face
    pair = 2

    def body(near_ref, ohi_ref, olo_ref, u_ref, in_ref, *refs):
        halo_refs, out_ref, x_ref = refs[:-2], refs[-2], refs[-1]
        core = spot()[2]
        lane = iota((SUB, E), 1)
        index = lax.axis_index("space") * E + lane
        total = sz.N * E
        back = index - jnp.broadcast_to(near_ref[0:1, :], (SUB, E))
        back = jnp.where(back < 0, back + total, back)
        front = jnp.broadcast_to(near_ref[1:2, :], (SUB, E)) - index
        front = jnp.where(front < 0, front + total, front)
        own_back = (lane + E - back) % E
        own_front = (lane + front) % E
        from_back = lane < back
        from_front = lane >= E - front
        first_core = core == 0
        tiles = face // SUB
        for l in range(L):
            at = pl.ds(l * SUB, SUB)
            if len(halo_refs) == 2:
                swap_ref, halo_ref = halo_refs
                prev_halo = jnp.where(first_core, halo_ref[at, :], swap_ref[sz.half, at, :])
                next_halo = jnp.where(first_core, swap_ref[sz.half + 1, at, :], halo_ref[at, :])
            else:
                sib_ref, ahead_ref, behind_ref = halo_refs
                prev_halo = jnp.where(first_core, behind_ref[at, :], sib_ref[at, :])
                next_halo = jnp.where(first_core, sib_ref[pl.ds(sz.H + l * SUB, SUB), :], ahead_ref[at, :])
            for k in range(FR // SUB):
                row = (k // tiles) * Q + (k % tiles) * SUB
                here = lanes_of(u_ref[l, pl.ds(row + Q - face, SUB), :], own_back)
                there = lanes_of(prev_halo, (REACH * k + REACH + lane + E - back) % E)
                x_ref[pl.ds(k * SUB, SUB), pl.ds(l * E, E)] = jnp.where(from_back, there, here)
                here = lanes_of(u_ref[l, pl.ds(row, SUB), :], own_front)
                there = lanes_of(next_halo, (REACH * k + lane + front) % E)
                x_ref[pl.ds(FR + k * SUB, SUB), pl.ds(l * E, E)] = jnp.where(from_front, there, here)
        for l in range(0, L, pair):
            x = x_ref[:, pl.ds(l * E, pair * E)]
            r = dot3(ohi_ref[:, : 2 * FR], olo_ref[:, : 2 * FR], x)
            for i in range(pair):
                out_ref[l + i] = in_ref[l + i] + r[:, i * E : (i + 1) * E]

    out = jax.ShapeDtypeStruct(u.shape, F32)
    flops = 12 * sz.R * FR * L * E
    ins = [VMEM] * (5 + len(halos))
    scratch = [pltpu.VMEM((2 * FR, L * E), F32)]
    args = (neighbours, *mats[2:], u, inner, *halos)
    return call(body, [out], ins, scratch, flops, 12 * u.size)(*args)[0]


def turn_time(sz, parts, damp=False, carried=()):
    weights = [float(w) for w in time_weights(sz.T)]
    T, L, M = sz.T, sz.L, sz.M
    rows = parts[0].shape[1]
    padded = -(-rows // SUB) * SUB
    front = carried[0].shape[1] if carried else 0

    def body(*refs):
        ins, fronts, outs, x_ref, y_ref = refs[:M], refs[M : M + len(carried)], refs[-2 - M : -2], refs[-2], refs[-1]
        me = spot()[0]
        for j in range(len(carried)):
            outs[j][:, pl.ds(0, front), :] = fronts[j][...]
        for j in range(M):
            x_ref[pl.ds((me ^ j) * L, L), pl.ds(0, rows), :] = ins[j][...]

        def some(i, carry):
            at = pl.ds(pl.multiple_of(i * SUB, SUB), SUB)
            x = [x_ref[t, at, :] for t in range(T)]
            diff = {}
            for t in range(T):
                total = None
                for k in range(1, T // 2):
                    a, b = (t + k) % T, (t - k) % T
                    if (a, b) not in diff and (b, a) not in diff:
                        diff[(a, b)] = x[a] - x[b]
                    term = weights[k] * diff[(a, b)] if (a, b) in diff else -weights[k] * diff[(b, a)]
                    total = term if total is None else total + term
                y_ref[t, at, :] = x[t] - STEP * total if damp else total
            return carry

        lax.fori_loop(0, padded // SUB, some, 0)
        for j in range(M):
            outs[j][:, pl.ds(front, rows), :] = y_ref[pl.ds((me ^ j) * L, L), pl.ds(0, rows), :]

    full = pltpu.VMEM((T, padded, sz.E), F32)
    size = T * rows * sz.E
    ins = [VMEM] * (M + len(carried))
    shapes = tm_shapes(sz, front + rows)
    return call(body, shapes, ins, [full, full], 20 * size, 8 * size)(*parts, *carried)


def shift_slide(sz, groups, shifts, keep, swapped, mine, theirs):
    Z, N, CH, E, half = sz.Z, sz.N, sz.CH, sz.E, sz.half

    def body(group_ref, shift_ref, keep_ref, swap_ref, *refs):
        a, b, outs, x_ref = refs[:half], refs[half : 2 * half], refs[2 * half : -1], refs[-1]
        _, z, core = spot()
        other = 1 - core
        l = z // sz.PL
        group, shift = group_ref[l], shift_ref[l]
        x_ref[2 * z + core] = keep_ref[0]
        x_ref[2 * z + other] = swap_ref[0]
        for j in range(1, half):
            one, two = pl.ds(sz.front(j), CH), pl.ds(sz.front(j) + CH, CH)
            chip = sz.ahead(z, other, j)
            x_ref[2 * chip + core] = a[j - 1][one, :]
            x_ref[2 * chip + other] = a[j - 1][two, :]
            chip = sz.ahead(z, core, j)
            x_ref[2 * chip + other] = b[j - 1][one, :]
            x_ref[2 * chip + core] = b[j - 1][two, :]
        far = lax.rem(z + half, Z)
        x_ref[2 * far + core] = a[half - 1][...]
        x_ref[2 * far + other] = b[half - 1][...]
        lane = iota((CH, E), 1)
        index = (lane + shift) % E

        def block(chip, which):
            first = 2 * chip + which + group
            near = x_ref[lax.rem(first, N)]
            return lanes_of(jnp.where(lane < shift, x_ref[lax.rem(first + 1, N)], near), index)

        outs[0][...] = block(z, core)
        for j in range(1, half):
            chip = sz.ahead(z, core, j)
            outs[j][pl.ds(0, CH), :] = block(chip, core)
            outs[j][pl.ds(CH, CH), :] = block(chip, other)
        outs[half][...] = block(far, core)

    single = jax.ShapeDtypeStruct((CH, E), F32)
    double = jax.ShapeDtypeStruct((2 * CH, E), F32)
    ins = [SMEM, SMEM] + [VMEM] * (2 + 2 * half)
    scratch = [pltpu.VMEM((N, CH, E), F32)]
    outs = [single] + [double] * (half - 1) + [single]
    return call(body, outs, ins, scratch, 0, 12 * N * CH * E)(groups, shifts, keep, swapped, *mine, *theirs)


def slide_rows(sz, slides, stage, x_ref, ring=False):
    E, face, FR, half = sz.E, sz.face, sz.FR, sz.half
    _, z, core = spot()
    if ring:
        for j in range(1, sz.Z):
            stage[lax.rem(z + sz.Z - j, sz.Z)] = slides[j][...]
    stage[z] = slides[0][...]
    for j in range(1, 0 if ring else half):
        stage[sz.ahead(z, 1 - core, j)] = slides[j][pl.ds(0, sz.CH), :]
        stage[sz.ahead(z, core, j)] = slides[half + j][pl.ds(sz.CH, sz.CH), :]
    if not ring:
        stage[lax.rem(z + half, sz.Z)] = slides[half][...]
    for l in range(sz.L):
        slide = [stage[l * sz.PL + i] for i in range(sz.PL)]
        slide = slide[0] if sz.PL == 1 else jnp.concatenate(slide, axis=0)
        cols = pl.ds(l * E, E)
        x_ref[:, cols] = slide
        v1 = slide[face : 2 * face]
        v2 = slide[2 * face : 3 * face]
        cosine, sine = turn_of(sz, l)
        x_ref[pl.ds(face, face), cols] = cosine * v1 - sine * v2
        x_ref[pl.ds(2 * face, face), cols] = sine * v1 + cosine * v2


def gather_rows(sz, parts, full):
    me = spot()[0]
    for j in range(sz.M):
        full[:, pl.ds(pl.multiple_of((me ^ j) * sz.RC, SUB), sz.RC), :] = parts[j][...]


def first_slide(sz, mats, u, local, slides):
    L, E, R, FR, M = sz.L, sz.E, sz.R, sz.FR, sz.M
    CR = FR // M
    pair = 2

    def body(ohi_ref, olo_ref, u_ref, w_ref, *refs):
        slide_refs, out_ref, chunks = refs[: sz.Z], refs[sz.Z], refs[sz.Z + 1 : sz.Z + 1 + M]
        stage, x_ref, cut_ref = refs[-3:]
        slide_rows(sz, slide_refs, stage, x_ref)
        for l in range(L):
            for m in range(M):
                cut_ref[m, l] = x_ref[pl.ds(m * CR, CR), pl.ds(l * E, E)]
        for j in range(M):
            chunks[j][...] = cut_ref[spot()[0] ^ j]
        for l in range(0, L, pair):
            outer = dot3(ohi_ref[:, 2 * FR :], olo_ref[:, 2 * FR :], x_ref[:, pl.ds(l * E, pair * E)])
            for i in range(pair):
                out_ref[l + i] = u_ref[l + i] - STEP * (w_ref[l + i] + outer[:, i * E : (i + 1) * E])

    outs = [jax.ShapeDtypeStruct(u.shape, F32)] + tm_shapes(sz, CR)
    scratch = [chip_scratch(sz), pltpu.VMEM((FR, L * E), F32), pltpu.VMEM((M, L, CR, E), F32)]
    ins = [VMEM] * (4 + sz.Z)
    done = call(body, outs, ins, scratch, 6 * R * FR * L * E, 12 * u.size)(*mats[2:], u, local, *slides)
    return done[0], done[1:]


def first_step(sz, partial, times):
    def body(c_ref, *refs):
        time_refs, u_ref, v_ref = refs[: sz.M], refs[sz.M], refs[sz.M + 1]
        zz, t_ref, stage = refs[sz.M + 2 : -2], refs[-2], refs[-1]
        gather_rows(sz, time_refs, t_ref)
        for l in range(sz.L):
            t = STEP * t_ref[l]
            new = c_ref[l] - t
            u_ref[l] = new
            v_ref[l] = new - t
        pack_ring(sz, u_ref, v_ref, zz, stage)

    full = jax.ShapeDtypeStruct(partial.shape, F32)
    scratch = [pltpu.VMEM(partial.shape, F32), chip_scratch(sz)]
    ins = [VMEM] * (1 + sz.M)
    done = call(body, [full, full] + ring_shapes(sz), ins, scratch, 0, 16 * partial.size)(partial, *times)
    return done[0], done[1], done[2:]


def last_step(sz, mats, u, local, times, slides):
    L, E, R, FR, M = sz.L, sz.E, sz.R, sz.FR, sz.M
    CR = FR // M
    pair = 2

    def body(ohi_ref, olo_ref, u_ref, w_ref, *refs):
        time_refs, refs = refs[:M], refs[M:]
        slide_refs, refs = refs[: sz.Z], refs[sz.Z :]
        new_ref, res_ref, t_ref, stage, x_ref, cut_ref = refs
        me = spot()[0]
        for j in range(M):
            t_ref[me ^ j] = time_refs[j][:, pl.ds(0, sz.RC), :]
            cut_ref[me ^ j] = time_refs[j][:, pl.ds(sz.RC, CR), :]
        slide_rows(sz, slide_refs, stage, x_ref, ring=True)
        for l in range(L):
            for m in range(M):
                x_ref[pl.ds(m * CR, CR), pl.ds(l * E, E)] -= STEP * cut_ref[m, l]
        for l in range(0, L, pair):
            outer = dot3(ohi_ref[:, 2 * FR :], olo_ref[:, 2 * FR :], x_ref[:, pl.ds(l * E, pair * E)])
            for i in range(pair):
                for m in range(M):
                    rows = slice(m * sz.RC, (m + 1) * sz.RC)
                    r = outer[rows, i * E : (i + 1) * E] + w_ref[l + i, rows] + t_ref[m, l + i]
                    new_ref[l + i, rows] = u_ref[l + i, rows] - STEP * r
                    res_ref[l + i, rows] = r

    full = jax.ShapeDtypeStruct(u.shape, F32)
    scratch = [pltpu.VMEM((M, L, sz.RC, E), F32)]
    scratch += [chip_scratch(sz), pltpu.VMEM((FR, L * E), F32), pltpu.VMEM((M, L, CR, E), F32)]
    ins = [VMEM] * (4 + M + sz.Z)
    args = (*mats[2:], u, local, *times, *slides)
    return call(body, [full, full], ins, scratch, 6 * R * FR * L * E, 20 * u.size)(*args)


def over_tm(x, j):
    size = lax.axis_size("tm")
    return lax.ppermute(x, "tm", [(i, i ^ j) for i in range(size)])


def over_chips(x, j):
    size = lax.axis_size("space")
    pairs = [(i, (i + (2 * j if i % 2 == 0 else -2 * j)) % size) for i in range(size)]
    return lax.ppermute(x, "space", pairs)


def over_ring(x, j):
    size = lax.axis_size("space")
    return lax.ppermute(x, "space", [(i, (i + 2 * j) % size) for i in range(size)])


def over_cores(x):
    size = lax.axis_size("space")
    return lax.ppermute(x, "space", [(i, i ^ 1) for i in range(size)])


def per_device(conserved_field, face_neighbours, counterpart_group, counterpart_shift, volume_operator, flux_matrix):
    sz = Sizes(conserved_field.shape)
    u = conserved_field.reshape(sz.L, sz.R, sz.E)

    def time_trip(parts):
        return [parts[0]] + [over_tm(parts[j], j) for j in range(1, sz.M)]

    def ring_trip(parts):
        return [parts[0]] + [over_ring(parts[j], j) for j in range(1, sz.Z)]

    chunks = pack_time(sz, u)
    parts = time_trip(chunks)
    swap, keep, far = pack_space(sz, after(u, chunks[0]))
    swapped = over_cores(swap)
    joined = join_cores(sz, keep, swapped)
    mine = [over_chips(joined[j - 1], j) for j in range(1, sz.half)] + [over_chips(far, sz.half)]
    mats = matrices(sz, after(flux_matrix, joined[0]), volume_operator)
    inner = inside_part(sz, mats, u)
    theirs = [over_cores(x) for x in after(mine, inner)]
    shifted = shift_slide(sz, counterpart_group, counterpart_shift, keep, swapped, mine, theirs)
    slides = [shifted[0]] + [over_chips(shifted[j], j) for j in range(1, sz.half + 1)]
    slides += [over_cores(x) for x in slides[1 : sz.half]]
    turned = turn_time(sz, after(parts, shifted[0]))
    times = time_trip(turned)
    here = face_part(sz, face_neighbours, mats, after(u, turned[0]), inner, swapped, mine[0])
    damped = turn_time(sz, after(turned, here), damp=True)
    partial, cuts = first_slide(sz, mats, u, after(here, damped), slides)
    cut_parts = time_trip(cuts)
    u, v, packed = first_step(sz, partial, times)
    mine = ring_trip(packed)
    inner = inside_part(sz, mats, v)
    both = turn_time(sz, after(cut_parts, inner), carried=damped)
    times = time_trip(both)
    theirs = [over_cores(x) for x in mine[:1] + after(mine[1:], both[0])]
    shifted = shift_ring(sz, counterpart_group, counterpart_shift, mine, theirs)
    slides = ring_trip(shifted)
    here = face_part(
        sz, face_neighbours, mats, after(v, shifted[0]), inner, theirs[0], theirs[sz.Z - 1], theirs[1]
    )
    new, residual = last_step(sz, mats, u, here, times, slides)
    shape = conserved_field.shape
    return new.reshape(shape), residual.reshape(shape)


def after(values, anchor):
    return lax.optimization_barrier((values, anchor))[0]


def solution(mesh):
    return jax.shard_map(
        per_device,
        mesh=mesh,
        in_specs=(P("tm", None, None, "space"), P(None, "space"), P("tm"), P("tm"), P(), P()),
        out_specs=(P("tm", None, None, "space"), P("tm", None, None, "space")),
        check_vma=False,
    )
```

```python
import functools

import jax
import jax.numpy as jnp
import numpy as np
from jax import lax
from jax.experimental import pallas as pl
from jax.experimental.pallas import tpu as pltpu
from jax.sharding import PartitionSpec as P

REACH = 4
LIFT = 2.0
DISSIPATION = 1.5
ANGULAR = 0.5
DAMPING = 4.0
STEP = 0.2
SUB = 8

VMEM = pl.BlockSpec(memory_space=pltpu.VMEM)
SMEM = pl.BlockSpec(memory_space=pltpu.SMEM)
F32 = jnp.float32
BF16 = jnp.bfloat16


class Sizes:
    def __init__(self, field_shape):
        self.L, self.V, self.Q, self.E = field_shape
        self.R = self.V * self.Q
        self.M = lax.axis_size("tm")
        self.N = lax.axis_size("space")
        self.T = self.L * self.M
        self.Z = self.N // 2
        self.half = self.Z // 2
        self.RC = self.R // self.M
        self.face = self.Q // 4
        self.FR = self.V * self.face
        self.PL = self.Z // self.L
        self.CH = self.FR // self.PL
        self.H = SUB * self.L

    def z_rows(self, j):
        if j == 0:
            return 2 * self.H + self.CH
        return self.CH + self.H * ((j == 1) + (j == self.Z - 1))

    def front(self, j):
        return self.H if j == 1 else 0

    def ahead(self, z, core, j):
        return lax.rem(z + self.Z + jnp.where(core == 0, j, -j), self.Z)


def time_weights(total):
    k = np.arange(1, total // 2, dtype=np.float64)
    gains = 2.0 * ANGULAR * k * np.exp(-DAMPING * (k / (total // 2)) ** 8) / total
    lag = np.arange(total, dtype=np.float64)
    return np.sum(gains[:, None] * np.sin(2.0 * np.pi * k[:, None] * lag[None, :] / total), axis=0)


def call(body, outs, ins, scratch=(), flops=0, nbytes=0):
    return pl.pallas_call(
        body,
        out_shape=outs,
        in_specs=ins,
        out_specs=jax.tree.map(lambda _: VMEM, outs),
        scratch_shapes=list(scratch),
        cost_estimate=pl.CostEstimate(flops=flops, bytes_accessed=nbytes, transcendentals=0),
        compiler_params=pltpu.CompilerParams(vmem_limit_bytes=16 * 1024 * 1024),
    )


def spot():
    s = lax.axis_index("space")
    return lax.axis_index("tm"), s // 2, lax.rem(s, 2)


def turn_of(sz, l):
    me = lax.axis_index("tm")
    cosine, sine = jnp.float32(1.0), jnp.float32(0.0)
    for m in range(sz.M):
        azimuth = 2.0 * np.pi * (m * sz.L + l) / sz.T
        cosine = jnp.where(me == m, jnp.float32(np.cos(azimuth)), cosine)
        sine = jnp.where(me == m, jnp.float32(np.sin(azimuth)), sine)
    return cosine, sine


def lanes_of(x, index):
    return jnp.take_along_axis(x, index, axis=1, mode="promise_in_bounds")


def split(x):
    hi = x.astype(BF16)
    return hi, (x - hi.astype(F32)).astype(BF16)


def dot3(a_hi, a_lo, x):
    x_hi, x_lo = split(x)
    out = jnp.dot(a_hi, x_hi, preferred_element_type=F32)
    out += jnp.dot(a_hi, x_lo, preferred_element_type=F32)
    return out + jnp.dot(a_lo, x_hi, preferred_element_type=F32)


def iota(shape, axis):
    return lax.broadcasted_iota(jnp.int32, shape, axis)


def matrices(sz, flux, volume_operator):
    V, Q, face = sz.V, sz.Q, sz.face

    def body(flux_ref, vol_ref, in_hi, in_lo, out_hi, out_lo):
        p = iota((Q, Q), 0)
        q = iota((Q, Q), 1)
        same = p == q
        low = same & (p < face)
        up = same & (p >= Q - face)
        slide = same & (p % 4 == 3)
        fp = iota((Q, face), 0)
        fq = iota((Q, face), 1)
        to_low = fp == fq
        to_up = fp == fq + (Q - face)
        to_slide = fp == 4 * fq + 3
        vol0 = vol_ref[0]
        vol1 = vol_ref[1]
        for v in range(V):
            blocks = []
            lows, ups, slides = [], [], []
            for w in range(V):
                f0 = flux_ref[0, v, w]
                f1 = flux_ref[1, v, w]
                d = DISSIPATION if v == w else 0.0
                a_low = 0.5 * LIFT * (-f0 - d)
                a_up = 0.5 * LIFT * (f0 - d)
                a_slide = 0.5 * LIFT * (f1 - d)
                block = f0 * vol0 + f1 * vol1
                block -= jnp.where(low, a_low, 0.0)
                block -= jnp.where(up, a_up, 0.0)
                block -= jnp.where(slide, a_slide, 0.0)
                blocks.append(block)
                lows.append(jnp.where(to_low, a_low, 0.0))
                ups.append(jnp.where(to_up, a_up, 0.0))
                slides.append(jnp.where(to_slide, a_slide, 0.0))
            hi, lo = split(jnp.concatenate(blocks, axis=1))
            in_hi[pl.ds(v * Q, Q), :] = hi
            in_lo[pl.ds(v * Q, Q), :] = lo
            hi, lo = split(jnp.concatenate(lows + ups + slides, axis=1))
            out_hi[pl.ds(v * Q, Q), :] = hi
            out_lo[pl.ds(v * Q, Q), :] = lo

    inner = jax.ShapeDtypeStruct((sz.R, sz.R), BF16)
    outer = jax.ShapeDtypeStruct((sz.R, 3 * sz.FR), BF16)
    nbytes = 4 * sz.R * (sz.R + 3 * sz.FR)
    return call(body, [inner, inner, outer, outer], [SMEM, VMEM], (), nbytes, nbytes)(flux, volume_operator)


def tm_shapes(sz, rows):
    return [jax.ShapeDtypeStruct((sz.L, rows, sz.E), F32) for _ in range(sz.M)]


def chip_shapes(sz):
    block = (sz.CH, sz.E)
    return [
        jax.ShapeDtypeStruct((sz.half + 2, *block), F32),
        jax.ShapeDtypeStruct((sz.half, *block), F32),
        jax.ShapeDtypeStruct(block, F32),
    ]


def pack_time(sz, u):
    def body(u_ref, *refs):
        outs, sems = refs[: sz.M], refs[-1]
        me = lax.axis_index("tm")
        copies = []
        for j in list(range(1, sz.M)) + [0]:
            start = pl.multiple_of((me ^ j) * sz.RC, SUB)
            copies.append(pltpu.make_async_copy(u_ref.at[:, pl.ds(start, sz.RC), :], outs[j], sems.at[j]))
            copies[-1].start()
        for copy in copies:
            copy.wait()

    scratch = [pltpu.SemaphoreType.DMA((sz.M,))]
    source = pl.BlockSpec(memory_space=pltpu.HBM)
    return call(body, tm_shapes(sz, sz.RC), [source], scratch, 0, 8 * u.size)(u)


def chip_scratch(sz):
    return pltpu.VMEM((sz.Z, sz.CH, sz.E), F32)


def pack_chips(sz, slide_ref, halo_ref, outs, stage):
    swap_ref, keep_ref, far_ref = outs
    _, z, core = spot()
    for p in range(sz.Z):
        first = (p % sz.PL) * sz.CH
        stage[p] = slide_ref[p // sz.PL, pl.ds(3 + 4 * first, sz.CH, stride=4), :]
    for j in range(sz.half):
        swap_ref[j] = stage[sz.ahead(z, 1 - core, j)]
        keep_ref[j] = stage[sz.ahead(z, core, j)]
    far_ref[...] = stage[lax.rem(z + sz.half, sz.Z)]
    lane = iota((SUB, sz.E), 1)
    slot = lane // REACH
    last = sz.E - REACH + lane % REACH
    first = lane % REACH
    tiles = sz.face // SUB
    for l in range(sz.L):
        up = jnp.zeros((SUB, sz.E), F32)
        low = jnp.zeros((SUB, sz.E), F32)
        for k in range(sz.FR // SUB):
            row = (k // tiles) * sz.Q + (k % tiles) * SUB
            up = jnp.where(slot == k, lanes_of(halo_ref[l, pl.ds(row + sz.Q - sz.face, SUB), :], last), up)
            low = jnp.where(slot == k, lanes_of(halo_ref[l, pl.ds(row, SUB), :], first), low)
        swap_ref[sz.half, pl.ds(l * SUB, SUB), :] = up
        swap_ref[sz.half + 1, pl.ds(l * SUB, SUB), :] = low


def ring_shapes(sz):
    return [jax.ShapeDtypeStruct((sz.z_rows(j), sz.E), F32) for j in range(sz.Z)]


def pack_ring(sz, slide_ref, halo_ref, zz, stage):
    z = spot()[1]
    for p in range(sz.Z):
        first = (p % sz.PL) * sz.CH
        stage[p] = slide_ref[p // sz.PL, pl.ds(3 + 4 * first, sz.CH, stride=4), :]
    lane = iota((SUB, sz.E), 1)
    slot = lane // REACH
    last = sz.E - REACH + lane % REACH
    first = lane % REACH
    tiles = sz.face // SUB
    halos = []
    for l in range(sz.L):
        up = jnp.zeros((SUB, sz.E), F32)
        low = jnp.zeros((SUB, sz.E), F32)
        for k in range(sz.FR // SUB):
            row = (k // tiles) * sz.Q + (k % tiles) * SUB
            up = jnp.where(slot == k, lanes_of(halo_ref[l, pl.ds(row + sz.Q - sz.face, SUB), :], last), up)
            low = jnp.where(slot == k, lanes_of(halo_ref[l, pl.ds(row, SUB), :], first), low)
        halos.append((up, low))
    for j in range(sz.Z):
        at = 0
        for which, wanted in ((0, j in (0, 1)), (1, j in (0, sz.Z - 1))):
            if wanted:
                for l in range(sz.L):
                    zz[j][pl.ds(at, SUB), :] = halos[l][which]
                    at += SUB
        zz[j][pl.ds(at, sz.CH), :] = stage[lax.rem(z + j, sz.Z)]


def shift_ring(sz, groups, shifts, mine, theirs):
    Z, N, CH, E = sz.Z, sz.N, sz.CH, sz.E

    def body(group_ref, shift_ref, *refs):
        a, b, outs, x_ref = refs[:Z], refs[Z : 2 * Z], refs[2 * Z : 3 * Z], refs[-1]
        _, z, core = spot()
        l = z // sz.PL
        group, shift = group_ref[l], shift_ref[l]
        for j in range(Z):
            chip = lax.rem(z + Z - j, Z)
            skip = sz.z_rows(j) - CH
            x_ref[2 * chip + core] = a[j][pl.ds(skip, CH), :]
            x_ref[2 * chip + 1 - core] = b[j][pl.ds(skip, CH), :]
        lane = iota((CH, E), 1)
        index = (lane + shift) % E
        for j in range(Z):
            block = 2 * lax.rem(z + j, Z) + core
            near = x_ref[lax.rem(block + group, N)]
            far = x_ref[lax.rem(block + group + 1, N)]
            outs[j][...] = lanes_of(jnp.where(lane < shift, far, near), index)

    out = jax.ShapeDtypeStruct((CH, E), F32)
    ins = [SMEM, SMEM] + [VMEM] * (2 * Z)
    scratch = [pltpu.VMEM((N, CH, E), F32)]
    return call(body, [out] * Z, ins, scratch, 0, 12 * N * CH * E)(groups, shifts, *mine, *theirs)


def join_cores(sz, keep, swapped):
    def body(keep_ref, swap_ref, *outs):
        core = spot()[2]
        for j in range(1, sz.half):
            out, front = outs[j - 1], sz.front(j)
            if front:
                out[pl.ds(0, front), :] = swap_ref[sz.half + core, pl.ds(0, front), :]
            out[pl.ds(front, sz.CH), :] = keep_ref[j]
            out[pl.ds(front + sz.CH, sz.CH), :] = swap_ref[j]

    shapes = [jax.ShapeDtypeStruct((sz.front(j) + 2 * sz.CH, sz.E), F32) for j in range(1, sz.half)]
    return call(body, shapes, [VMEM, VMEM], (), 0, 16 * sz.half * sz.CH * sz.E)(keep, swapped)


def pack_space(sz, u):
    def body(u_ref, *refs):
        held, sem = refs[-2], refs[-1]
        copy = pltpu.make_async_copy(u_ref, held, sem)
        copy.start()
        copy.wait()
        pack_chips(sz, held, held, refs[:-3], refs[-3])

    scratch = [chip_scratch(sz), pltpu.VMEM(u.shape, F32), pltpu.SemaphoreType.DMA]
    source = pl.BlockSpec(memory_space=pltpu.HBM)
    return call(body, chip_shapes(sz), [source], scratch, 0, 4 * u.size)(u)


def inside_part(sz, mats, u):
    E, pair = sz.E, 2

    def body(hi_ref, lo_ref, u_ref, out_ref):
        for l in range(0, sz.L, pair):
            x = jnp.concatenate([u_ref[l + i] for i in range(pair)], axis=1)
            r = dot3(hi_ref[...], lo_ref[...], x)
            for i in range(pair):
                out_ref[l + i] = r[:, i * E : (i + 1) * E]

    out = jax.ShapeDtypeStruct(u.shape, F32)
    return call(body, [out], [VMEM] * 3, (), 6 * sz.R * u.size, 12 * u.size)(*mats[:2], u)[0]


def face_part(sz, neighbours, mats, u, inner, *halos):
    L, E, FR, Q, face = sz.L, sz.E, sz.FR, sz.Q, sz.face
    pair = 2

    def body(near_ref, ohi_ref, olo_ref, u_ref, in_ref, *refs):
        halo_refs, out_ref, x_ref = refs[:-2], refs[-2], refs[-1]
        core = spot()[2]
        lane = iota((SUB, E), 1)
        index = lax.axis_index("space") * E + lane
        total = sz.N * E
        back = index - jnp.broadcast_to(near_ref[0:1, :], (SUB, E))
        back = jnp.where(back < 0, back + total, back)
        front = jnp.broadcast_to(near_ref[1:2, :], (SUB, E)) - index
        front = jnp.where(front < 0, front + total, front)
        own_back = (lane + E - back) % E
        own_front = (lane + front) % E
        from_back = lane < back
        from_front = lane >= E - front
        first_core = core == 0
        tiles = face // SUB
        for l in range(L):
            at = pl.ds(l * SUB, SUB)
            if len(halo_refs) == 2:
                swap_ref, halo_ref = halo_refs
                prev_halo = jnp.where(first_core, halo_ref[at, :], swap_ref[sz.half, at, :])
                next_halo = jnp.where(first_core, swap_ref[sz.half + 1, at, :], halo_ref[at, :])
            else:
                sib_ref, ahead_ref, behind_ref = halo_refs
                prev_halo = jnp.where(first_core, behind_ref[at, :], sib_ref[at, :])
                next_halo = jnp.where(first_core, sib_ref[pl.ds(sz.H + l * SUB, SUB), :], ahead_ref[at, :])
            for k in range(FR // SUB):
                row = (k // tiles) * Q + (k % tiles) * SUB
                here = lanes_of(u_ref[l, pl.ds(row + Q - face, SUB), :], own_back)
                there = lanes_of(prev_halo, (REACH * k + REACH + lane + E - back) % E)
                x_ref[pl.ds(k * SUB, SUB), pl.ds(l * E, E)] = jnp.where(from_back, there, here)
                here = lanes_of(u_ref[l, pl.ds(row, SUB), :], own_front)
                there = lanes_of(next_halo, (REACH * k + lane + front) % E)
                x_ref[pl.ds(FR + k * SUB, SUB), pl.ds(l * E, E)] = jnp.where(from_front, there, here)
        for l in range(0, L, pair):
            x = x_ref[:, pl.ds(l * E, pair * E)]
            r = dot3(ohi_ref[:, : 2 * FR], olo_ref[:, : 2 * FR], x)
            for i in range(pair):
                out_ref[l + i] = in_ref[l + i] + r[:, i * E : (i + 1) * E]

    out = jax.ShapeDtypeStruct(u.shape, F32)
    flops = 12 * sz.R * FR * L * E
    ins = [VMEM] * (5 + len(halos))
    scratch = [pltpu.VMEM((2 * FR, L * E), F32)]
    args = (neighbours, *mats[2:], u, inner, *halos)
    return call(body, [out], ins, scratch, flops, 12 * u.size)(*args)[0]


def turn_time(sz, parts, damp=False, carried=()):
    weights = [float(w) for w in time_weights(sz.T)]
    T, L, M = sz.T, sz.L, sz.M
    rows = parts[0].shape[1]
    padded = -(-rows // SUB) * SUB
    front = carried[0].shape[1] if carried else 0

    def body(*refs):
        ins, fronts, outs, x_ref, y_ref = refs[:M], refs[M : M + len(carried)], refs[-2 - M : -2], refs[-2], refs[-1]
        me = spot()[0]
        for j in range(len(carried)):
            outs[j][:, pl.ds(0, front), :] = fronts[j][...]
        for j in range(M):
            x_ref[pl.ds((me ^ j) * L, L), pl.ds(0, rows), :] = ins[j][...]

        def some(i, carry):
            at = pl.ds(pl.multiple_of(i * SUB, SUB), SUB)
            x = [x_ref[t, at, :] for t in range(T)]
            diff = {}
            for t in range(T):
                total = None
                for k in range(1, T // 2):
                    a, b = (t + k) % T, (t - k) % T
                    if (a, b) not in diff and (b, a) not in diff:
                        diff[(a, b)] = x[a] - x[b]
                    term = weights[k] * diff[(a, b)] if (a, b) in diff else -weights[k] * diff[(b, a)]
                    total = term if total is None else total + term
                y_ref[t, at, :] = x[t] - STEP * total if damp else total
            return carry

        lax.fori_loop(0, padded // SUB, some, 0)
        for j in range(M):
            outs[j][:, pl.ds(front, rows), :] = y_ref[pl.ds((me ^ j) * L, L), pl.ds(0, rows), :]

    full = pltpu.VMEM((T, padded, sz.E), F32)
    size = T * rows * sz.E
    ins = [VMEM] * (M + len(carried))
    shapes = tm_shapes(sz, front + rows)
    return call(body, shapes, ins, [full, full], 20 * size, 8 * size)(*parts, *carried)


def shift_slide(sz, groups, shifts, keep, swapped, mine, theirs):
    Z, N, CH, E, half = sz.Z, sz.N, sz.CH, sz.E, sz.half

    def body(group_ref, shift_ref, keep_ref, swap_ref, *refs):
        a, b, outs, x_ref = refs[:half], refs[half : 2 * half], refs[2 * half : -1], refs[-1]
        _, z, core = spot()
        other = 1 - core
        l = z // sz.PL
        group, shift = group_ref[l], shift_ref[l]
        x_ref[2 * z + core] = keep_ref[0]
        x_ref[2 * z + other] = swap_ref[0]
        for j in range(1, half):
            one, two = pl.ds(sz.front(j), CH), pl.ds(sz.front(j) + CH, CH)
            chip = sz.ahead(z, other, j)
            x_ref[2 * chip + core] = a[j - 1][one, :]
            x_ref[2 * chip + other] = a[j - 1][two, :]
            chip = sz.ahead(z, core, j)
            x_ref[2 * chip + other] = b[j - 1][one, :]
            x_ref[2 * chip + core] = b[j - 1][two, :]
        far = lax.rem(z + half, Z)
        x_ref[2 * far + core] = a[half - 1][...]
        x_ref[2 * far + other] = b[half - 1][...]
        lane = iota((CH, E), 1)
        index = (lane + shift) % E

        def block(chip, which):
            first = 2 * chip + which + group
            near = x_ref[lax.rem(first, N)]
            return lanes_of(jnp.where(lane < shift, x_ref[lax.rem(first + 1, N)], near), index)

        outs[0][...] = block(z, core)
        for j in range(1, half):
            chip = sz.ahead(z, core, j)
            outs[j][pl.ds(0, CH), :] = block(chip, core)
            outs[j][pl.ds(CH, CH), :] = block(chip, other)
        outs[half][...] = block(far, core)

    single = jax.ShapeDtypeStruct((CH, E), F32)
    double = jax.ShapeDtypeStruct((2 * CH, E), F32)
    ins = [SMEM, SMEM] + [VMEM] * (2 + 2 * half)
    scratch = [pltpu.VMEM((N, CH, E), F32)]
    outs = [single] + [double] * (half - 1) + [single]
    return call(body, outs, ins, scratch, 0, 12 * N * CH * E)(groups, shifts, keep, swapped, *mine, *theirs)


def slide_rows(sz, slides, stage, x_ref, ring=False):
    E, face, FR, half = sz.E, sz.face, sz.FR, sz.half
    _, z, core = spot()
    if ring:
        for j in range(1, sz.Z):
            stage[lax.rem(z + sz.Z - j, sz.Z)] = slides[j][...]
    stage[z] = slides[0][...]
    for j in range(1, 0 if ring else half):
        stage[sz.ahead(z, 1 - core, j)] = slides[j][pl.ds(0, sz.CH), :]
        stage[sz.ahead(z, core, j)] = slides[half + j][pl.ds(sz.CH, sz.CH), :]
    if not ring:
        stage[lax.rem(z + half, sz.Z)] = slides[half][...]
    for l in range(sz.L):
        slide = [stage[l * sz.PL + i] for i in range(sz.PL)]
        slide = slide[0] if sz.PL == 1 else jnp.concatenate(slide, axis=0)
        cols = pl.ds(l * E, E)
        x_ref[:, cols] = slide
        v1 = slide[face : 2 * face]
        v2 = slide[2 * face : 3 * face]
        cosine, sine = turn_of(sz, l)
        x_ref[pl.ds(face, face), cols] = cosine * v1 - sine * v2
        x_ref[pl.ds(2 * face, face), cols] = sine * v1 + cosine * v2


def gather_rows(sz, parts, full):
    me = spot()[0]
    for j in range(sz.M):
        full[:, pl.ds(pl.multiple_of((me ^ j) * sz.RC, SUB), sz.RC), :] = parts[j][...]


def first_slide(sz, mats, u, local, slides):
    L, E, R, FR, M = sz.L, sz.E, sz.R, sz.FR, sz.M
    CR = FR // M
    pair = 2

    def body(ohi_ref, olo_ref, u_ref, w_ref, *refs):
        slide_refs, out_ref, chunks = refs[: sz.Z], refs[sz.Z], refs[sz.Z + 1 : sz.Z + 1 + M]
        stage, x_ref, cut_ref = refs[-3:]
        slide_rows(sz, slide_refs, stage, x_ref)
        for l in range(L):
            for m in range(M):
                cut_ref[m, l] = x_ref[pl.ds(m * CR, CR), pl.ds(l * E, E)]
        for j in range(M):
            chunks[j][...] = cut_ref[spot()[0] ^ j]
        for l in range(0, L, pair):
            outer = dot3(ohi_ref[:, 2 * FR :], olo_ref[:, 2 * FR :], x_ref[:, pl.ds(l * E, pair * E)])
            for i in range(pair):
                out_ref[l + i] = u_ref[l + i] - STEP * (w_ref[l + i] + outer[:, i * E : (i + 1) * E])

    outs = [jax.ShapeDtypeStruct(u.shape, F32)] + tm_shapes(sz, CR)
    scratch = [chip_scratch(sz), pltpu.VMEM((FR, L * E), F32), pltpu.VMEM((M, L, CR, E), F32)]
    ins = [VMEM] * (4 + sz.Z)
    done = call(body, outs, ins, scratch, 6 * R * FR * L * E, 12 * u.size)(*mats[2:], u, local, *slides)
    return done[0], done[1:]


def first_step(sz, partial, times):
    def body(c_ref, *refs):
        time_refs, u_ref, v_ref = refs[: sz.M], refs[sz.M], refs[sz.M + 1]
        zz, t_ref, stage = refs[sz.M + 2 : -2], refs[-2], refs[-1]
        gather_rows(sz, time_refs, t_ref)
        for l in range(sz.L):
            t = STEP * t_ref[l]
            new = c_ref[l] - t
            u_ref[l] = new
            v_ref[l] = new - t
        pack_ring(sz, u_ref, v_ref, zz, stage)

    full = jax.ShapeDtypeStruct(partial.shape, F32)
    scratch = [pltpu.VMEM(partial.shape, F32), chip_scratch(sz)]
    ins = [VMEM] * (1 + sz.M)
    done = call(body, [full, full] + ring_shapes(sz), ins, scratch, 0, 16 * partial.size)(partial, *times)
    return done[0], done[1], done[2:]


def last_step(sz, mats, u, local, times, slides):
    L, E, R, FR, M = sz.L, sz.E, sz.R, sz.FR, sz.M
    CR = FR // M
    pair = 2

    def body(ohi_ref, olo_ref, u_ref, w_ref, *refs):
        time_refs, refs = refs[:M], refs[M:]
        slide_refs, refs = refs[: sz.Z], refs[sz.Z :]
        new_ref, res_ref, t_ref, stage, x_ref, cut_ref = refs
        me = spot()[0]
        for j in range(M):
            t_ref[me ^ j] = time_refs[j][:, pl.ds(0, sz.RC), :]
            cut_ref[me ^ j] = time_refs[j][:, pl.ds(sz.RC, CR), :]
        slide_rows(sz, slide_refs, stage, x_ref, ring=True)
        for l in range(L):
            for m in range(M):
                x_ref[pl.ds(m * CR, CR), pl.ds(l * E, E)] -= STEP * cut_ref[m, l]
        for l in range(0, L, pair):
            outer = dot3(ohi_ref[:, 2 * FR :], olo_ref[:, 2 * FR :], x_ref[:, pl.ds(l * E, pair * E)])
            for i in range(pair):
                for m in range(M):
                    rows = slice(m * sz.RC, (m + 1) * sz.RC)
                    r = outer[rows, i * E : (i + 1) * E] + w_ref[l + i, rows] + t_ref[m, l + i]
                    new_ref[l + i, rows] = u_ref[l + i, rows] - STEP * r
                    res_ref[l + i, rows] = r

    full = jax.ShapeDtypeStruct(u.shape, F32)
    scratch = [pltpu.VMEM((M, L, sz.RC, E), F32)]
    scratch += [chip_scratch(sz), pltpu.VMEM((FR, L * E), F32), pltpu.VMEM((M, L, CR, E), F32)]
    ins = [VMEM] * (4 + M + sz.Z)
    args = (*mats[2:], u, local, *times, *slides)
    return call(body, [full, full], ins, scratch, 6 * R * FR * L * E, 20 * u.size)(*args)


def over_tm(x, j):
    size = lax.axis_size("tm")
    return lax.ppermute(x, "tm", [(i, i ^ j) for i in range(size)])


def over_chips(x, j):
    size = lax.axis_size("space")
    pairs = [(i, (i + (2 * j if i % 2 == 0 else -2 * j)) % size) for i in range(size)]
    return lax.ppermute(x, "space", pairs)


def over_ring(x, j):
    size = lax.axis_size("space")
    return lax.ppermute(x, "space", [(i, (i + 2 * j) % size) for i in range(size)])


def over_cores(x):
    size = lax.axis_size("space")
    return lax.ppermute(x, "space", [(i, i ^ 1) for i in range(size)])


def per_device(conserved_field, face_neighbours, counterpart_group, counterpart_shift, volume_operator, flux_matrix):
    sz = Sizes(conserved_field.shape)
    u = conserved_field.reshape(sz.L, sz.R, sz.E)

    def time_trip(parts):
        moved = {j: over_tm(parts[j], j) for j in reversed(range(1, sz.M))}
        return [parts[0]] + [moved[j] for j in range(1, sz.M)]

    def ring_trip(parts):
        return [parts[0]] + [over_ring(parts[j], j) for j in range(1, sz.Z)]

    chunks = pack_time(sz, u)
    parts = time_trip(chunks)
    swap, keep, far = pack_space(sz, after(u, chunks[0]))
    swapped = over_cores(swap)
    joined = join_cores(sz, keep, swapped)
    mine = [over_chips(joined[j - 1], j) for j in range(1, sz.half)] + [over_chips(far, sz.half)]
    mats = matrices(sz, after(flux_matrix, joined[0]), volume_operator)
    inner = inside_part(sz, mats, u)
    theirs = [over_cores(x) for x in after(mine, inner)]
    shifted = shift_slide(sz, counterpart_group, counterpart_shift, keep, swapped, mine, theirs)
    slides = [shifted[0]] + [over_chips(shifted[j], j) for j in range(1, sz.half + 1)]
    slides += [over_cores(x) for x in slides[1 : sz.half]]
    turned = turn_time(sz, after(parts, shifted[0]))
    times = time_trip(turned)
    here = face_part(sz, face_neighbours, mats, after(u, turned[0]), inner, swapped, mine[0])
    damped = turn_time(sz, after(turned, here), damp=True)
    partial, cuts = first_slide(sz, mats, u, after(here, damped), slides)
    cut_parts = time_trip(cuts)
    u, v, packed = first_step(sz, partial, times)
    mine = ring_trip(packed)
    inner = inside_part(sz, mats, v)
    both = turn_time(sz, after(cut_parts, inner), carried=damped)
    times = time_trip(both)
    theirs = [over_cores(x) for x in mine[:1] + after(mine[1:], both[0])]
    shifted = shift_ring(sz, counterpart_group, counterpart_shift, mine, theirs)
    slides = ring_trip(shifted)
    here = face_part(
        sz, face_neighbours, mats, after(v, shifted[0]), inner, theirs[0], theirs[sz.Z - 1], theirs[1]
    )
    new, residual = last_step(sz, mats, u, here, times, slides)
    shape = conserved_field.shape
    return new.reshape(shape), residual.reshape(shape)


def after(values, anchor):
    return lax.optimization_barrier((values, anchor))[0]


def solution(mesh):
    return jax.shard_map(
        per_device,
        mesh=mesh,
        in_specs=(P("tm", None, None, "space"), P(None, "space"), P("tm"), P("tm"), P(), P()),
        out_specs=(P("tm", None, None, "space"), P("tm", None, None, "space")),
        check_vma=False,
    )
```
